32 devices in a mesh: replica: 2 (over y), expert: 4 (over z), dp: 4 (over x, core).
Axes of the slice: x: 2, y: 2, z: 4, core: 2. Of those that a mesh axis runs over, the one named last changes fastest.
Arguments:
- queries: bfloat16 [192, 2, 4096], P(('replica', 'expert', 'dp')), parts along dimension 0, may hold values from -128 to 128
- new_keys: bfloat16 [192, 2, 256], P(('replica', 'expert', 'dp')), parts along dimension 0, may hold values from -6 to 6
- new_values: bfloat16 [192, 2, 256], P(('replica', 'expert', 'dp')), parts along dimension 0, may hold values from -6 to 6
- cache_keys: bfloat16 [192, 32, 256], P(('replica', 'expert', 'dp')), parts along dimension 0, may hold values from -6 to 6
- cache_values: bfloat16 [192, 32, 256], P(('replica', 'expert', 'dp')), parts along dimension 0, may hold values from -6 to 6
- lengths: int32 [192], P(('replica', 'expert', 'dp')), parts along dimension 0, may hold values from 18 to 32, as said below
- image_grid: int32 [192, 2], P(('replica', 'expert', 'dp')), parts along dimension 0, may hold values from 1 to 4
- residual: bfloat16 [192, 2, 4096], P(('replica', 'expert', 'dp')), parts along dimension 0, may hold values from -6 to 6
- norm_gain: bfloat16 [4096], replicated, may hold values from 0.5 to 2
- routes: int32 [192, 2, 8], P(('replica', 'expert', 'dp')), parts along dimension 0, may hold values from 0 to 63, all different within a row; in each aligned block of 12 rows (0 to 11, 12 to 23, ..., all dimensions but the last counted through in order) at most 2 rows name the same one
- route_gains: float32 [192, 2, 8], P(('replica', 'expert', 'dp')), parts along dimension 0, may hold values from 0.1 to 1
- w_gate: bfloat16 [64, 4096, 768], P('expert', None, 'dp'), may hold values from -0.09375 to 0.09375
- w_up: bfloat16 [64, 4096, 768], P('expert', None, 'dp'), may hold values from -0.09375 to 0.09375
- w_down: bfloat16 [64, 768, 4096], P('expert', 'dp'), may hold values from -0.21875 to 0.21875
Outputs:
- layer_out: bfloat16 [192, 2, 4096], P(('replica', 'expert', 'dp')), parts along dimension 0
The draws below stay inside these ranges and needn't reach their ends.
There are 2 independent parts, one for each index of `replica`. The reference program is written for one: setup_inputs(seed, part) draws one part's arguments, and reference() takes and returns one part's arrays. A program takes and returns all parts, laid end to end along the dimension named above; an argument that names none is the same for every part. Nothing has to cross between parts.
Inputs may be any that keep to these rules, and one draw needn't show every extreme that they name: `routes`: each row names 8 different experts at each step. In the rows of one device (aligned blocks of 6 rows, both steps together) no expert is named more than 2 times. `lengths`: every row's cache holds its image tokens and at least two more live positions.
All inputs are finite; a program needn't handle non-finite values.
Results may differ from the reference program's by a relative error of at most 0.008.
Values may be sent and summed in bfloat16 or wider, within the bound.
No kernel may reach another device: no remote copies, remote signals or barrier semaphores. Data moves between devices by JAX's collectives and lax.ppermute only.
A program may use at most 192 MiB of HBM per device.

```python
import math
import jax
import jax.numpy as jnp
import numpy as np
from jax import lax

D = 4096
HEADS = 32
KV_HEADS = 2
HEAD_DIM = 128
EXPERTS = 64
EXPERT_FF = 768
TOP = 8
CAP = 2
STEPS = 2
GRID = 4
CTX = 32
ROWS_DEV = 6
ROWS = 96
N_EXPERT = 4
N_DP = 4


THETA = 5000000.0


LIMIT = 128.0


def rotate_drawn(vectors, where):
    half = vectors.shape[-1] // 2
    freq = THETA ** (-2.0 * jnp.arange(half, dtype=jnp.float32) / vectors.shape[-1])
    angle = where[..., None] * freq
    cosine = jnp.cos(angle)
    sine = jnp.sin(angle)
    first = vectors[..., :half]
    second = vectors[..., half:]
    return jnp.concatenate([first * cosine - second * sine, second * cosine + first * sine], axis=-1)


def layout(key):
    key = jax.random.fold_in(key, 101)
    first, second, third, fourth = jax.random.split(key, 4)
    places = jnp.arange(ROWS, dtype=jnp.int32)
    widest = jax.random.randint(third, (), 0, ROWS, dtype=jnp.int32)
    narrow = (widest + 1 + jax.random.randint(fourth, (), 0, ROWS - 1, dtype=jnp.int32)) % ROWS
    grid = jax.random.randint(first, (ROWS, 2), 1, GRID + 1, dtype=jnp.int32)
    grid = jnp.where((places == widest)[:, None], GRID, grid)
    grid = jnp.where((places == narrow)[:, None], 1, grid)
    lengths = jax.random.randint(second, (ROWS,), GRID * GRID + 2, CTX + 1, dtype=jnp.int32)
    lengths = jnp.where(places == narrow, CTX, lengths)
    return (lengths, grid)


def attention_draw(key, strength):
    lengths, grid = layout(key)
    base = lengths - grid[:, 0] * grid[:, 1] + jnp.maximum(grid[:, 0], grid[:, 1])
    key = jax.random.fold_in(key, 202)
    key_query, key_fresh, key_cache, key_pick, key_target = jax.random.split(key, 5)
    group = HEADS // KV_HEADS
    queries = jnp.clip(jax.random.normal(key_query, (ROWS, STEPS, HEADS, HEAD_DIM), jnp.float32), -6.0, 6.0)
    fresh = jnp.clip(jax.random.normal(key_fresh, (ROWS, STEPS, KV_HEADS, HEAD_DIM), jnp.float32), -6.0, 6.0)
    cached = jnp.clip(jax.random.normal(key_cache, (ROWS, CTX, KV_HEADS, HEAD_DIM), jnp.float32), -6.0, 6.0)
    chosen = jax.random.bernoulli(key_pick, 0.25, (ROWS, 1, 1, 1)).astype(jnp.float32) * strength
    target = jax.random.uniform(key_target, (ROWS, STEPS, HEADS, 1), jnp.float32, 110.0, 340.0)
    aligned = jnp.clip(target * HEAD_DIM ** (-0.5) * jnp.repeat(fresh, group, axis=2), -LIMIT, LIMIT)
    queries = queries * (1.0 - chosen) + aligned * chosen
    where = (base[:, None] + jnp.arange(STEPS, dtype=jnp.int32)[None, :]).astype(jnp.float32)
    twin = jnp.clip(rotate_drawn(fresh, where[:, :, None]) * (1.0 + 1.0 / 120.0), -6.0, 6.0)
    front = cached[:, :STEPS] * (1.0 - chosen) + twin * chosen
    cached = jnp.concatenate([front, cached[:, STEPS:]], axis=1)
    return (queries.reshape(ROWS, STEPS, HEADS * HEAD_DIM), fresh.reshape(ROWS, STEPS, KV_HEADS * HEAD_DIM), cached.reshape(ROWS, CTX, KV_HEADS * HEAD_DIM))


def draw_queries(key, part):
    strength = 0.0
    return attention_draw(key, strength)[0].astype(jnp.bfloat16)


def draw_new_keys(key, part):
    strength = 0.0
    return attention_draw(key, strength)[1].astype(jnp.bfloat16)


def draw_cache_keys(key, part):
    strength = 0.0
    return attention_draw(key, strength)[2].astype(jnp.bfloat16)


def draw_lengths(key, part):
    return layout(key)[0]


def draw_image_grid(key, part):
    return layout(key)[1]


def block_scale(key, dims, pieces, smallest, largest):
    factor_of, own = 1.0, jax.random.fold_in(key, 6)
    for dim, blocks in pieces:
        draws = jnp.exp(jax.random.uniform(jax.random.fold_in(own, dim), (blocks,), jnp.float32, smallest / len(pieces), largest / len(pieces)))
        factor_of = factor_of * jnp.repeat(draws, dims[dim] // blocks).reshape([-1 if axis == dim else 1 for axis in range(len(dims))])
    return factor_of


def shared_out(key, own, number, rows, number_of, top, limit, slope):
    ranking = jax.random.permutation(key, number_of)
    packed, usual = portions_of(number_of, rows * top, limit, slope, True), portions_of(number_of, rows * top, limit, slope, False)
    places = jnp.arange(number_of)

    def named(sizes, offset_by):
        used = int((sizes > 0).sum())
        fixed = max(1, used // 4)
        passed = fixed + (places - fixed + offset_by * (used - fixed)) % max(1, number_of - fixed)
        return jnp.zeros((number_of,), jnp.int32).at[ranking[jnp.where(places < fixed, places, passed)]].set(jnp.asarray(sizes, jnp.int32))

    sizes = jnp.where(number % 4 == 0, named(packed, number // 4), named(usual, number - number // 4 - 1))
    mixed = jax.random.permutation(jax.random.fold_in(own, 3), number_of)
    donor, sink = mixed[0:number_of // 2 * 2:2], mixed[1:number_of // 2 * 2:2]
    slack = jnp.minimum(sizes[donor] - 1, limit - sizes[sink]) // 2
    slack = jnp.where((donor == ranking[0]) | (sink == ranking[0]) | (sizes[sink] == 0), 0, jnp.maximum(slack, 0))
    passed = jax.random.randint(jax.random.fold_in(own, 4), (number_of // 2,), 0, 1 << 20) % (slack + 1)
    sizes = sizes.at[donor].add(-passed).at[sink].add(passed)
    labels = jnp.searchsorted(jnp.cumsum(sizes), jnp.arange(rows * top), side="right").astype(jnp.int32)
    listing = labels.reshape(top, rows).T
    listing = listing[jax.random.permutation(jax.random.fold_in(own, 1), rows)]
    offset_by = jax.random.randint(jax.random.fold_in(own, 2), (rows, 1), 0, top)
    return jnp.take_along_axis(listing, (jnp.arange(top)[None, :] + offset_by) % top, axis=1)


def portions_of(count, total, bound, lean, full):
    portions = [(1 << 20) // math.isqrt(rank ** lean) + 1 for rank in range(1, count + 1)]
    largest = bound if full else min(bound, max(-(-total // count), total * portions[0] // sum(portions)))
    least = 1 if total - largest >= count - 1 else 0
    given, spare = [largest] + [least] * (count - 1), total - largest - least * (count - 1)
    while spare > 0:
        movable = [i for i in range(1, count) if given[i] < largest] or [i for i in range(1, count) if given[i] < bound]
        mass, remaining = sum([portions[i] for i in movable]), spare
        for i in movable:
            extra = min(bound - given[i], max(1, remaining * portions[i] // mass), spare)
            given[i] = given[i] + extra
            spare = spare - extra
    return np.array(given)


def bell_draw(stream_key, extent, scale, reach, cuts=(), held_as=jnp.bfloat16):
    values = scale * jax.random.normal(stream_key, extent, jnp.float32)
    if cuts:
        values = values * block_scale(stream_key, extent, cuts, -0.22, 0.18)
    return jnp.clip(values, -reach, reach).astype(held_as)


def setup_inputs(seed: int = 0, part: int = 0) -> dict:
    arg_keys = jax.random.split(jax.random.key(seed), 15)
    own_keys = jax.random.split(jax.random.fold_in(arg_keys[14], part), 15)
    queries = draw_queries(jax.random.fold_in(jax.random.fold_in(arg_keys[14], part), 71), part)
    new_keys = draw_new_keys(jax.random.fold_in(jax.random.fold_in(arg_keys[14], part), 71), part)
    new_values = bell_draw(own_keys[2], (ROWS, STEPS, KV_HEADS * HEAD_DIM), 1.0, 6.0, ((0, 16),))
    cache_keys = draw_cache_keys(jax.random.fold_in(jax.random.fold_in(arg_keys[14], part), 71), part)
    cache_values = bell_draw(own_keys[4], (ROWS, CTX, KV_HEADS * HEAD_DIM), 1.0, 6.0, ((0, 16),))
    lengths = draw_lengths(jax.random.fold_in(jax.random.fold_in(arg_keys[14], part), 71), part)
    image_grid = draw_image_grid(jax.random.fold_in(jax.random.fold_in(arg_keys[14], part), 71), part)
    residual = bell_draw(own_keys[7], (ROWS, STEPS, D), 1.0, 6.0, ((0, 16),))
    norm_gain = jnp.clip(jnp.exp(jax.random.uniform(arg_keys[8], (D,), jnp.float32, math.log(0.5), math.log(2.0))), 0.5, 2.0).astype(jnp.bfloat16)
    routes_keys = jax.random.split(jax.random.fold_in(own_keys[9], 1), ROWS * STEPS // (ROWS_DEV * STEPS))
    routes_turns = jax.random.permutation(jax.random.fold_in(own_keys[9], 3), ROWS * STEPS // (ROWS_DEV * STEPS))
    routes = jax.vmap(lambda own, number: shared_out(jax.random.fold_in(own_keys[9], 2), own, number, ROWS_DEV * STEPS, EXPERTS, TOP, CAP, 2))(routes_keys, routes_turns).reshape((ROWS, STEPS, TOP))
    route_gains = jnp.clip(jnp.exp(math.log(1.0) - 2.3025851 * jax.random.uniform(own_keys[10], (ROWS, STEPS, TOP), jnp.float32) ** block_scale(own_keys[10], (ROWS, STEPS, TOP), ((0, 16),), -0.2, 0.2)), 0.1, 1.0)
    w_gate = bell_draw(arg_keys[11], (EXPERTS, D, EXPERT_FF), D ** -0.5, 0.09375, ((0, 4), (2, 4)))
    w_up = bell_draw(arg_keys[12], (EXPERTS, D, EXPERT_FF), D ** -0.5, 0.09375, ((0, 4), (2, 4)))
    w_down = bell_draw(arg_keys[13], (EXPERTS, EXPERT_FF, D), EXPERT_FF ** -0.5, 0.21875, ((0, 4), (1, 4)))
    return {"queries": queries, "new_keys": new_keys, "new_values": new_values, "cache_keys": cache_keys, "cache_values": cache_values, "lengths": lengths, "image_grid": image_grid, "residual": residual, "norm_gain": norm_gain, "routes": routes, "route_gains": route_gains, "w_gate": w_gate, "w_up": w_up, "w_down": w_down}


THETA = 5000000.0
EPS = 1e-06
MASKED = -1e+30

def rotate(vectors, where):
    half = vectors.shape[-1] // 2
    freq = THETA ** (-2.0 * jnp.arange(half, dtype=jnp.float32) / vectors.shape[-1])
    angle = where[..., None] * freq
    cosine = jnp.cos(angle)
    sine = jnp.sin(angle)
    first = vectors[..., :half]
    second = vectors[..., half:]
    return jnp.concatenate([first * cosine - second * sine, second * cosine + first * sine], axis=-1)

def attend(queries, new_keys, new_values, cache_keys, cache_values, lengths, image_grid):
    count = queries.shape[0]
    steps = queries.shape[1]
    ctx = cache_keys.shape[1]
    kv_count = cache_keys.shape[2] // HEAD_DIM
    group = queries.shape[2] // HEAD_DIM // kv_count
    base = lengths - image_grid[:, 0] * image_grid[:, 1] + jnp.maximum(image_grid[:, 0], image_grid[:, 1])
    where = (base[:, None] + jnp.arange(steps, dtype=jnp.int32)[None, :]).astype(jnp.float32)
    query = rotate(queries.astype(jnp.float32).reshape(count, steps, kv_count, group, HEAD_DIM), where[:, :, None, None])
    fresh = rotate(new_keys.astype(jnp.float32).reshape(count, steps, kv_count, HEAD_DIM), where[:, :, None])
    cached = cache_keys.astype(jnp.float32).reshape(count, ctx, kv_count, HEAD_DIM)
    scale = 1.0 / math.sqrt(HEAD_DIM)
    old_scores = jnp.einsum('rsgqd,rcgd->rsgqc', query, cached, precision=lax.Precision.HIGHEST) * scale
    new_scores = jnp.einsum('rsgqd,rtgd->rsgqt', query, fresh, precision=lax.Precision.HIGHEST) * scale
    live = jnp.arange(ctx, dtype=jnp.int32)[None, :] < lengths[:, None]
    old_scores = jnp.where(live[:, None, None, None, :], old_scores, MASKED)
    causal = jnp.arange(steps, dtype=jnp.int32)[None, :] <= jnp.arange(steps, dtype=jnp.int32)[:, None]
    new_scores = jnp.where(causal[None, :, None, None, :], new_scores, MASKED)
    scores = jnp.concatenate([old_scores, new_scores], axis=-1)
    top = lax.optimization_barrier(jnp.max(scores, axis=-1, keepdims=True))
    weights = jnp.exp(scores - top)
    probs = (weights / lax.optimization_barrier(jnp.sum(weights, axis=-1, keepdims=True))).astype(jnp.bfloat16)
    values = jnp.concatenate([cache_values.reshape(count, ctx, kv_count, HEAD_DIM), new_values.reshape(count, steps, kv_count, HEAD_DIM)], axis=1)
    out = jnp.einsum('rsgqc,rcgd->rsgqd', probs.astype(jnp.float32), values.astype(jnp.float32))
    return out.astype(jnp.bfloat16).reshape(count, steps, -1)

def experts(normed, routes, shares, w_gate, w_up, w_down):
    flat = normed.reshape(-1, normed.shape[-1])
    picks = routes.reshape(-1).astype(jnp.int32)
    gains = shares.reshape(-1).astype(jnp.float32)
    total = picks.shape[0]
    order = jnp.argsort(picks, stable=True).astype(jnp.int32)
    counts = lax.optimization_barrier(jnp.sum((picks[:, None] == jnp.arange(EXPERTS, dtype=jnp.int32)[None, :]).astype(jnp.int32), axis=0)).astype(jnp.int32)
    starts = (jnp.cumsum(counts) - counts).astype(jnp.int32)
    bucket = CAP * N_EXPERT * N_DP
    quarter = EXPERT_FF // N_DP

    def visit(carry, item):
        gate_w, up_w, down_w, start, size = item
        slots = jnp.arange(bucket, dtype=jnp.int32)
        index = order[jnp.minimum(start + slots, total - 1)]
        valid = slots < size
        owner = (index // TOP).astype(jnp.int32)
        rows_in = flat[owner]
        gate = jnp.dot(rows_in, gate_w, preferred_element_type=jnp.float32)
        upper = jnp.dot(rows_in, up_w, preferred_element_type=jnp.float32)
        hidden = (jax.nn.silu(gate) * upper).astype(jnp.bfloat16)
        result = jnp.zeros((bucket, flat.shape[1]), jnp.float32)
        for block in range(N_DP):
            piece = jnp.dot(hidden[:, block * quarter:(block + 1) * quarter], down_w[block * quarter:(block + 1) * quarter], preferred_element_type=jnp.float32).astype(jnp.bfloat16)
            result = result + lax.optimization_barrier(piece).astype(jnp.float32)
        output = lax.optimization_barrier(result.astype(jnp.bfloat16)).astype(jnp.float32)
        contribution = jnp.where(valid[:, None], gains[index][:, None] * output, jnp.float32(0.0))
        return (carry.at[owner].add(contribution), None)
    summed, _ = lax.scan(visit, jnp.zeros(flat.shape, jnp.float32), (w_gate, w_up, w_down, starts, counts))
    return summed.reshape(normed.shape)

def reference(queries, new_keys, new_values, cache_keys, cache_values, lengths, image_grid, residual, norm_gain, routes, route_gains, w_gate, w_up, w_down):
    attended = attend(queries, new_keys, new_values, cache_keys, cache_values, lengths, image_grid)
    mixed = residual.astype(jnp.float32) + attended.astype(jnp.float32)
    normed = (mixed * lax.rsqrt(lax.optimization_barrier(jnp.mean(mixed * mixed, axis=-1, keepdims=True)) + EPS) * norm_gain.astype(jnp.float32)).astype(jnp.bfloat16)
    shares = (route_gains / lax.optimization_barrier(jnp.sum(route_gains, axis=-1, keepdims=True))).astype(jnp.bfloat16)
    routed = experts(normed, routes, shares, w_gate, w_up, w_down)
    return (mixed + routed).astype(jnp.bfloat16)
```

```python
import functools
import math

import jax
import jax.numpy as jnp
from jax import lax
from jax.experimental import pallas as pl
from jax.experimental.pallas import tpu as pltpu
from jax.sharding import PartitionSpec as P

HEAD_DIM = 128
TOP = 8
CAP = 2


THETA = 5000000.0
EPS = 1e-06
MASKED = -1e30


def rotate(vectors, where):
    half = vectors.shape[-1] // 2
    freq = THETA ** (-2.0 * jnp.arange(half, dtype=jnp.float32) / vectors.shape[-1])
    angle = where[..., None] * freq
    cosine = jnp.cos(angle)
    sine = jnp.sin(angle)
    first = vectors[..., :half]
    second = vectors[..., half:]
    return jnp.concatenate(
        [first * cosine - second * sine, second * cosine + first * sine], axis=-1
    )


def attend(queries, new_keys, new_values, cache_keys, cache_values, lengths, image_grid):
    count = queries.shape[0]
    steps = queries.shape[1]
    ctx = cache_keys.shape[1]
    kv_count = cache_keys.shape[2] // HEAD_DIM
    group = queries.shape[2] // HEAD_DIM // kv_count
    base = (
        lengths
        - image_grid[:, 0] * image_grid[:, 1]
        + jnp.maximum(image_grid[:, 0], image_grid[:, 1])
    )
    where = (base[:, None] + jnp.arange(steps, dtype=jnp.int32)[None, :]).astype(jnp.float32)
    query = rotate(
        queries.astype(jnp.float32).reshape(count, steps, kv_count, group, HEAD_DIM),
        where[:, :, None, None],
    )
    fresh = rotate(
        new_keys.astype(jnp.float32).reshape(count, steps, kv_count, HEAD_DIM), where[:, :, None]
    )
    cached = cache_keys.astype(jnp.float32).reshape(count, ctx, kv_count, HEAD_DIM)
    scale = 1.0 / math.sqrt(HEAD_DIM)
    old_scores = (
        jnp.einsum("rsgqd,rcgd->rsgqc", query, cached, precision=lax.Precision.HIGHEST) * scale
    )
    new_scores = (
        jnp.einsum("rsgqd,rtgd->rsgqt", query, fresh, precision=lax.Precision.HIGHEST) * scale
    )
    live = jnp.arange(ctx, dtype=jnp.int32)[None, :] < lengths[:, None]
    old_scores = jnp.where(live[:, None, None, None, :], old_scores, MASKED)
    causal = (
        jnp.arange(steps, dtype=jnp.int32)[None, :] <= jnp.arange(steps, dtype=jnp.int32)[:, None]
    )
    new_scores = jnp.where(causal[None, :, None, None, :], new_scores, MASKED)
    scores = jnp.concatenate([old_scores, new_scores], axis=-1)
    top = jnp.max(scores, axis=-1, keepdims=True)
    weights = jnp.exp(scores - top)
    probs = (weights / jnp.sum(weights, axis=-1, keepdims=True)).astype(jnp.bfloat16)
    values = jnp.concatenate(
        [
            cache_values.reshape(count, ctx, kv_count, HEAD_DIM),
            new_values.reshape(count, steps, kv_count, HEAD_DIM),
        ],
        axis=1,
    )
    out = jnp.einsum("rsgqc,rcgd->rsgqd", probs, values, preferred_element_type=jnp.float32)
    return out.astype(jnp.bfloat16).reshape(count, steps, -1)


def shards(
    queries,
    new_keys,
    new_values,
    cache_keys,
    cache_values,
    lengths,
    image_grid,
    residual,
    norm_gain,
    routes,
    route_gains,
    w_gate,
    w_up,
    w_down,
):
    rows, steps, width = residual.shape
    attended = attend(queries, new_keys, new_values, cache_keys, cache_values, lengths, image_grid)
    mixed = residual.astype(jnp.float32) + attended.astype(jnp.float32)
    normed = (
        mixed
        * lax.rsqrt(jnp.mean(mixed * mixed, axis=-1, keepdims=True) + EPS)
        * norm_gain.astype(jnp.float32)
    ).astype(jnp.bfloat16)
    shares = (route_gains / jnp.sum(route_gains, axis=-1, keepdims=True)).astype(jnp.bfloat16)
    members = lax.axis_size("expert")
    local = w_gate.shape[0]
    places = members * CAP * local
    picks = routes.reshape(-1)
    onehot = (picks[:, None] == jnp.arange(members * local, dtype=jnp.int32)[None, :]).astype(
        jnp.int32
    )
    earlier = jnp.sum((jnp.cumsum(onehot, axis=0) - onehot) * onehot, axis=1)
    target = picks // local * (CAP * local) + earlier * local + picks % local
    placed = (target[:, None] == jnp.arange(places, dtype=jnp.int32)[None, :]).reshape(
        rows * steps, TOP, places
    )
    chooser = jnp.sum(placed.astype(jnp.float32), axis=1).astype(jnp.bfloat16)
    weigher = jnp.sum(
        jnp.where(
            placed, shares.reshape(rows * steps, TOP, 1).astype(jnp.float32), jnp.float32(0.0)
        ),
        axis=1,
    ).astype(jnp.bfloat16)
    outgoing = jnp.einsum(
        "jp,jd->pd",
        chooser,
        normed.reshape(rows * steps, width),
        preferred_element_type=jnp.float32,
    )
    outgoing = outgoing.astype(jnp.bfloat16).reshape(members, CAP, local, width)
    incoming = lax.all_to_all(outgoing, "expert", split_axis=0, concat_axis=0, tiled=True)
    flat = incoming.reshape(-1, local, width)
    piece = lax.all_gather(flat, "dp", axis=0, tiled=True)
    gate = jnp.einsum("red,edh->reh", piece, w_gate, preferred_element_type=jnp.float32)
    upper = jnp.einsum("red,edh->reh", piece, w_up, preferred_element_type=jnp.float32)
    hidden = (jax.nn.silu(gate) * upper).astype(jnp.bfloat16)
    piece = hidden
    result = lax.psum_scatter(
        jnp.einsum("reh,ehd->red", piece, w_down, preferred_element_type=jnp.float32).astype(
            jnp.bfloat16
        ),
        "dp",
        scatter_dimension=0,
        tiled=True,
    )
    returned = lax.all_to_all(
        result.reshape(incoming.shape), "expert", split_axis=0, concat_axis=0, tiled=True
    )
    routed = jnp.dot(weigher, returned.reshape(places, width), preferred_element_type=jnp.float32)
    layer_out = mixed.reshape(rows * steps, width) + routed
    return layer_out.astype(jnp.bfloat16).reshape(rows, steps, width)


VMEM = pl.BlockSpec(memory_space=pltpu.VMEM)
SMEM = pl.BlockSpec(memory_space=pltpu.SMEM)
LANES = 128
MAIN = 8


def stack(parts, axis=0):
    return jnp.concatenate(parts, axis=axis)


def front_kernel(
    q_ref, nk_ref, nv_ref, ck_ref, cv_ref, len_ref, grid_ref, res_ref, gain_ref, routes_ref,
    gains_ref, pay_ref, mixed_ref,
):
    rows, steps, width = q_ref.shape
    ctx = ck_ref.shape[1]
    kv_count = ck_ref.shape[2] // HEAD_DIM
    group = width // HEAD_DIM // kv_count
    half = HEAD_DIM // 2
    tall = group * steps
    fresh_pad = 8
    keys = ctx + fresh_pad
    lane = lax.broadcasted_iota(jnp.int32, (8, HEAD_DIM), 1)
    freq = jnp.exp((lane % half).astype(jnp.float32) * (-2.0 * math.log(THETA) / HEAD_DIM))
    sub = lax.broadcasted_iota(jnp.int32, (8, HEAD_DIM), 0)
    flip = jnp.where(lane < half, -1.0, 1.0)
    head_step = lax.broadcasted_iota(jnp.int32, (tall, keys), 0) % steps
    column = lax.broadcasted_iota(jnp.int32, (tall, keys), 1)
    fresh_live = (column >= ctx) & (column - ctx <= head_step)
    scale = 1.0 / math.sqrt(HEAD_DIM)

    def turn(vectors, cosine, sine):
        return vectors * cosine + pltpu.roll(vectors, half, 1) * sine

    normed = []
    for r in range(rows):
        length = len_ref[r]
        high, wide = grid_ref[r, 0], grid_ref[r, 1]
        base = length - high * wide + jnp.maximum(high, wide)
        angle = (base + sub % steps).astype(jnp.float32) * freq
        cosine = jnp.cos(angle)
        sine = jnp.sin(angle) * flip
        cosines = stack([cosine] * (tall // 8))
        sines = stack([sine] * (tall // 8))
        live = (column < jnp.minimum(length, ctx)) | fresh_live
        q_r = q_ref[r].astype(jnp.float32)
        nk_r = nk_ref[r].astype(jnp.float32)
        nv_r = nv_ref[r].astype(jnp.float32)
        ck_r = ck_ref[r].astype(jnp.float32)
        cv_r = cv_ref[r].astype(jnp.float32)
        blank = jnp.zeros((fresh_pad - steps, HEAD_DIM), jnp.float32)
        pieces = []
        for g in range(kv_count):
            cols = slice(g * HEAD_DIM, (g + 1) * HEAD_DIM)
            first = g * group
            query = stack(
                [q_r[:, (first + h) * HEAD_DIM : (first + h + 1) * HEAD_DIM] for h in range(group)]
            )
            query = turn(query, cosines, sines)
            fresh = turn(stack([nk_r[:, cols], blank]), cosine, sine)
            key = stack([ck_r[:, cols], fresh])
            scores = (
                lax.dot_general(
                    query, key, (((1,), (1,)), ((), ())),
                    precision=lax.Precision.HIGHEST, preferred_element_type=jnp.float32,
                )
                * scale
            )
            scores = jnp.where(live, scores, MASKED)
            top = jnp.max(scores, axis=-1, keepdims=True)
            weights = jnp.exp(scores - top)
            probs = (weights / jnp.sum(weights, axis=-1, keepdims=True)).astype(jnp.bfloat16)
            value = stack([cv_r[:, cols], nv_r[:, cols], blank]).astype(jnp.bfloat16)
            out = jnp.dot(probs, value, preferred_element_type=jnp.float32)
            out = out.astype(jnp.bfloat16).astype(jnp.float32)
            pieces += [out[h * steps : (h + 1) * steps] for h in range(group)]
        mixed = res_ref[r].astype(jnp.float32) + stack(pieces, axis=1)
        mixed_ref[r] = mixed
        mean = jnp.mean(mixed * mixed, axis=-1, keepdims=True)
        normed.append(mixed * lax.rsqrt(mean + EPS) * gain_ref[...].astype(jnp.float32))

    whole = MAIN // steps
    fold = width // 2
    pay_ref[:, :width] = stack(normed[:whole]).astype(pay_ref.dtype)
    late = normed[whole:]
    pay_ref[:, width : width + fold] = stack(
        [n[:, :fold] for n in late] + [n[:, fold:] for n in late]
    ).astype(pay_ref.dtype)

    place = lax.broadcasted_iota(jnp.int32, (steps, LANES), 1)
    spread = []
    for r in range(rows):
        gains = gains_ref[r]
        shares = gains / jnp.sum(gains, axis=-1, keepdims=True)
        picks = routes_ref[r] + (0 if r < whole else LANES // 2)
        dense = jnp.zeros((steps, LANES), jnp.float32)
        for k in range(TOP):
            dense = jnp.where(place == picks[:, k : k + 1], shares[:, k : k + 1], dense)
        spread.append(dense)
    early = stack(spread[:whole])
    late = stack(spread[whole:] + [jnp.zeros((MAIN - (rows - whole) * steps, LANES), jnp.float32)])
    pay_ref[:, width + fold :] = (early + late).astype(pay_ref.dtype)


def front(queries, new_keys, new_values, cache_keys, cache_values, lengths, image_grid, residual,
          norm_gain, routes, route_gains):
    rows, steps, width = queries.shape
    return pl.pallas_call(
        front_kernel,
        out_shape=(
            jax.ShapeDtypeStruct((MAIN, width + width // 2 + LANES), jnp.bfloat16),
            jax.ShapeDtypeStruct((rows, steps, width), jnp.float32),
        ),
        in_specs=[VMEM] * 5 + [SMEM] * 2 + [VMEM] * 4,
        out_specs=(VMEM, VMEM),
        cost_estimate=pl.CostEstimate(flops=10**7, bytes_accessed=10**6, transcendentals=10**4),
    )(queries, new_keys, new_values, cache_keys, cache_values, lengths, image_grid, residual,
      norm_gain.reshape(1, width), routes, route_gains)


def experts_kernel(blocks, local, axis, *refs):
    pays = refs[:blocks]
    gate_ref, up_ref, down_ref, near_ref, far_ref, x_ref, share_ref, total_ref = refs[blocks:]
    step = pl.program_id(0)
    count, quarter, width = gate_ref.shape
    fold = width // 2
    rest = 4
    tokens = blocks * (MAIN + rest)

    @pl.when(step == 0)
    def _():
        for i in range(0, blocks, 2):
            pair = [pays[i + j][...].astype(jnp.float32) for j in range(2)]
            x_ref[i * MAIN : (i + 2) * MAIN] = stack([p[:, :width] for p in pair]).astype(x_ref.dtype)
            share_ref[i * MAIN : (i + 2) * MAIN] = stack([p[:, width + fold :] for p in pair])
        for i in range(0, blocks, 4):
            start = blocks * MAIN + i * rest
            four = [pays[i + j][...].astype(jnp.float32) for j in range(4)]
            left = stack([p[:rest, width : width + fold] for p in four])
            right = stack([p[rest:, width : width + fold] for p in four])
            x_ref[start : start + 4 * rest, :fold] = left.astype(x_ref.dtype)
            x_ref[start : start + 4 * rest, fold:] = right.astype(x_ref.dtype)
            share_ref[start : start + 4 * rest] = stack([p[:rest, width + fold :] for p in four])
        total_ref[...] = jnp.zeros_like(total_ref)

    first = lax.axis_index(axis) * local + step * count
    lane = lax.broadcasted_iota(jnp.int32, (tokens, LANES), 1)
    row = lax.broadcasted_iota(jnp.int32, (tokens, LANES), 0)
    offset = jnp.where(row < blocks * MAIN, 0, LANES // 2)
    shares = share_ref[...]
    flat = (((1,), (1,)), ((), ()))
    gate = lax.dot_general(
        x_ref[...], gate_ref[...].reshape(count * quarter, width), flat,
        preferred_element_type=jnp.float32,
    )
    upper = lax.dot_general(
        x_ref[...], up_ref[...].reshape(count * quarter, width), flat,
        preferred_element_type=jnp.float32,
    )
    hidden = jax.nn.silu(gate) * upper
    unit = lax.broadcasted_iota(jnp.int32, hidden.shape, 1)
    weight = jnp.zeros_like(hidden)
    for e in range(count):
        share = jnp.sum(jnp.where(lane == first + e + offset, shares, 0.0), axis=1, keepdims=True)
        weight = jnp.where((unit >= e * quarter) & (unit < (e + 1) * quarter), share, weight)
    hidden = (hidden * weight).astype(jnp.bfloat16)
    total_ref[...] += jnp.dot(
        hidden, down_ref[...].reshape(count * quarter, width), preferred_element_type=jnp.float32
    )

    @pl.when(step == pl.num_programs(0) - 1)
    def _():
        for b in range(blocks):
            out = near_ref if b < blocks // 2 else far_ref
            at = b % (blocks // 2)
            out[at, :, :width] = total_ref[b * MAIN : (b + 1) * MAIN].astype(out.dtype)
            start = blocks * MAIN + b * rest
            late = total_ref[start : start + rest]
            out[at, :, width:] = stack([late[:, :fold], late[:, fold:]]).astype(out.dtype)


def experts(pays, w_gate, w_up, w_down, axis, count):
    blocks = len(pays)
    local, quarter, width = w_down.shape
    tokens = blocks * 12
    packed = width + width // 2
    weights = pl.BlockSpec((count, quarter, width), lambda i: (i, 0, 0))
    half = jax.ShapeDtypeStruct((blocks // 2, MAIN, packed), jnp.bfloat16)
    return pl.pallas_call(
        functools.partial(experts_kernel, blocks, local, axis),
        grid=(local // count,),
        out_shape=(half, half),
        in_specs=[VMEM] * blocks + [weights] * 3,
        out_specs=(VMEM, VMEM),
        scratch_shapes=[
            pltpu.VMEM((tokens, width), jnp.bfloat16),
            pltpu.VMEM((tokens, LANES), jnp.float32),
            pltpu.VMEM((tokens, width), jnp.float32),
        ],
        compiler_params=pltpu.CompilerParams(vmem_limit_bytes=60 * 2**20),
        cost_estimate=pl.CostEstimate(
            flops=6 * tokens * local * quarter * width,
            bytes_accessed=6 * local * quarter * width,
            transcendentals=tokens * local * quarter,
        ),
    )(*pays, jnp.swapaxes(w_gate, 1, 2), jnp.swapaxes(w_up, 1, 2), w_down)


def final_kernel(mixed_ref, *refs):
    parts, out_ref = refs[:-1], refs[-1]
    rows, steps, width = mixed_ref.shape
    fold = width // 2
    total = parts[0][...].astype(jnp.float32)
    for part in parts[1:]:
        total = total + part[...].astype(jnp.float32)
    for r in range(rows):
        at = r * steps
        if at < MAIN:
            routed = total[at : at + steps, :width]
        else:
            at -= MAIN
            low = total[at : at + steps, width:]
            at += MAIN // 2
            routed = stack([low, total[at : at + steps, width:]], axis=1)
        out_ref[r] = (mixed_ref[r] + routed).astype(out_ref.dtype)


def gathered(
    queries, new_keys, new_values, cache_keys, cache_values, lengths, image_grid, residual,
    norm_gain, routes, route_gains, w_gate, w_up, w_down,
):
    members = lax.axis_size("expert")
    pay, mixed = front(
        queries, new_keys, new_values, cache_keys, cache_values, lengths, image_grid, residual,
        norm_gain, routes, route_gains,
    )
    twin = [(0, 1), (1, 0), (2, 3), (3, 2)]
    side = [(0, 2), (2, 0), (1, 3), (3, 1)]
    shifts = (2, 1, 3)
    ahead = {k: [(i, (i + k) % members) for i in range(members)] for k in shifts}
    back = {k: [(i, (i - k) % members) for i in range(members)] for k in shifts}
    line = [pay] + [lax.ppermute(pay, "expert", ahead[k]) for k in shifts]
    pays = line + [lax.ppermute(p, "dp", side) for p in line]
    pays = pays + [lax.ppermute(p, "dp", twin) for p in pays]
    near, far = experts(pays, w_gate, w_up, w_down, "expert", 4)
    far = lax.ppermute(far, "dp", twin)
    near = (near.astype(jnp.float32) + far.astype(jnp.float32)).astype(jnp.bfloat16)
    peer = lax.ppermute(near[members:], "dp", side)
    near = (near[:members].astype(jnp.float32) + peer.astype(jnp.float32)).astype(jnp.bfloat16)
    parts = [near[0]] + [
        lax.ppermute(near[i + 1], "expert", back[k]) for i, k in enumerate(shifts)
    ]
    return pl.pallas_call(
        final_kernel,
        out_shape=jax.ShapeDtypeStruct(residual.shape, jnp.bfloat16),
        in_specs=[VMEM] * (1 + members),
        out_specs=VMEM,
    )(mixed, *parts)


def solution(mesh):
    placed = (
        P(("replica", "expert", "dp"), None, None),
        P(("replica", "expert", "dp"), None, None),
        P(("replica", "expert", "dp"), None, None),
        P(("replica", "expert", "dp"), None, None),
        P(("replica", "expert", "dp"), None, None),
        P(("replica", "expert", "dp")),
        P(("replica", "expert", "dp"), None),
        P(("replica", "expert", "dp"), None, None),
        P(),
        P(("replica", "expert", "dp"), None, None),
        P(("replica", "expert", "dp"), None, None),
        P("expert", None, "dp"),
        P("expert", None, "dp"),
        P("expert", "dp", None),
    )
    near = mesh.shape["expert"] == 4 and mesh.shape["dp"] == 4
    return jax.shard_map(
        gathered if near else shards,
        mesh=mesh,
        in_specs=placed,
        out_specs=P(("replica", "expert", "dp"), None, None),
        check_vma=False,
    )
```

```python
import functools
import math

import jax
import jax.numpy as jnp
from jax import lax
from jax.experimental import pallas as pl
from jax.experimental.pallas import tpu as pltpu
from jax.sharding import PartitionSpec as P

HEAD_DIM = 128
TOP = 8
CAP = 2


THETA = 5000000.0
EPS = 1e-06
MASKED = -1e30


def rotate(vectors, where):
    half = vectors.shape[-1] // 2
    freq = THETA ** (-2.0 * jnp.arange(half, dtype=jnp.float32) / vectors.shape[-1])
    angle = where[..., None] * freq
    cosine = jnp.cos(angle)
    sine = jnp.sin(angle)
    first = vectors[..., :half]
    second = vectors[..., half:]
    return jnp.concatenate(
        [first * cosine - second * sine, second * cosine + first * sine], axis=-1
    )


def attend(queries, new_keys, new_values, cache_keys, cache_values, lengths, image_grid):
    count = queries.shape[0]
    steps = queries.shape[1]
    ctx = cache_keys.shape[1]
    kv_count = cache_keys.shape[2] // HEAD_DIM
    group = queries.shape[2] // HEAD_DIM // kv_count
    base = (
        lengths
        - image_grid[:, 0] * image_grid[:, 1]
        + jnp.maximum(image_grid[:, 0], image_grid[:, 1])
    )
    where = (base[:, None] + jnp.arange(steps, dtype=jnp.int32)[None, :]).astype(jnp.float32)
    query = rotate(
        queries.astype(jnp.float32).reshape(count, steps, kv_count, group, HEAD_DIM),
        where[:, :, None, None],
    )
    fresh = rotate(
        new_keys.astype(jnp.float32).reshape(count, steps, kv_count, HEAD_DIM), where[:, :, None]
    )
    cached = cache_keys.astype(jnp.float32).reshape(count, ctx, kv_count, HEAD_DIM)
    scale = 1.0 / math.sqrt(HEAD_DIM)
    old_scores = (
        jnp.einsum("rsgqd,rcgd->rsgqc", query, cached, precision=lax.Precision.HIGHEST) * scale
    )
    new_scores = (
        jnp.einsum("rsgqd,rtgd->rsgqt", query, fresh, precision=lax.Precision.HIGHEST) * scale
    )
    live = jnp.arange(ctx, dtype=jnp.int32)[None, :] < lengths[:, None]
    old_scores = jnp.where(live[:, None, None, None, :], old_scores, MASKED)
    causal = (
        jnp.arange(steps, dtype=jnp.int32)[None, :] <= jnp.arange(steps, dtype=jnp.int32)[:, None]
    )
    new_scores = jnp.where(causal[None, :, None, None, :], new_scores, MASKED)
    scores = jnp.concatenate([old_scores, new_scores], axis=-1)
    top = jnp.max(scores, axis=-1, keepdims=True)
    weights = jnp.exp(scores - top)
    probs = (weights / jnp.sum(weights, axis=-1, keepdims=True)).astype(jnp.bfloat16)
    values = jnp.concatenate(
        [
            cache_values.reshape(count, ctx, kv_count, HEAD_DIM),
            new_values.reshape(count, steps, kv_count, HEAD_DIM),
        ],
        axis=1,
    )
    out = jnp.einsum("rsgqc,rcgd->rsgqd", probs, values, preferred_element_type=jnp.float32)
    return out.astype(jnp.bfloat16).reshape(count, steps, -1)


def shards(
    queries,
    new_keys,
    new_values,
    cache_keys,
    cache_values,
    lengths,
    image_grid,
    residual,
    norm_gain,
    routes,
    route_gains,
    w_gate,
    w_up,
    w_down,
):
    rows, steps, width = residual.shape
    attended = attend(queries, new_keys, new_values, cache_keys, cache_values, lengths, image_grid)
    mixed = residual.astype(jnp.float32) + attended.astype(jnp.float32)
    normed = (
        mixed
        * lax.rsqrt(jnp.mean(mixed * mixed, axis=-1, keepdims=True) + EPS)
        * norm_gain.astype(jnp.float32)
    ).astype(jnp.bfloat16)
    shares = (route_gains / jnp.sum(route_gains, axis=-1, keepdims=True)).astype(jnp.bfloat16)
    members = lax.axis_size("expert")
    local = w_gate.shape[0]
    places = members * CAP * local
    picks = routes.reshape(-1)
    onehot = (picks[:, None] == jnp.arange(members * local, dtype=jnp.int32)[None, :]).astype(
        jnp.int32
    )
    earlier = jnp.sum((jnp.cumsum(onehot, axis=0) - onehot) * onehot, axis=1)
    target = picks // local * (CAP * local) + earlier * local + picks % local
    placed = (target[:, None] == jnp.arange(places, dtype=jnp.int32)[None, :]).reshape(
        rows * steps, TOP, places
    )
    chooser = jnp.sum(placed.astype(jnp.float32), axis=1).astype(jnp.bfloat16)
    weigher = jnp.sum(
        jnp.where(
            placed, shares.reshape(rows * steps, TOP, 1).astype(jnp.float32), jnp.float32(0.0)
        ),
        axis=1,
    ).astype(jnp.bfloat16)
    outgoing = jnp.einsum(
        "jp,jd->pd",
        chooser,
        normed.reshape(rows * steps, width),
        preferred_element_type=jnp.float32,
    )
    outgoing = outgoing.astype(jnp.bfloat16).reshape(members, CAP, local, width)
    incoming = lax.all_to_all(outgoing, "expert", split_axis=0, concat_axis=0, tiled=True)
    flat = incoming.reshape(-1, local, width)
    piece = lax.all_gather(flat, "dp", axis=0, tiled=True)
    gate = jnp.einsum("red,edh->reh", piece, w_gate, preferred_element_type=jnp.float32)
    upper = jnp.einsum("red,edh->reh", piece, w_up, preferred_element_type=jnp.float32)
    hidden = (jax.nn.silu(gate) * upper).astype(jnp.bfloat16)
    piece = hidden
    result = lax.psum_scatter(
        jnp.einsum("reh,ehd->red", piece, w_down, preferred_element_type=jnp.float32).astype(
            jnp.bfloat16
        ),
        "dp",
        scatter_dimension=0,
        tiled=True,
    )
    returned = lax.all_to_all(
        result.reshape(incoming.shape), "expert", split_axis=0, concat_axis=0, tiled=True
    )
    routed = jnp.dot(weigher, returned.reshape(places, width), preferred_element_type=jnp.float32)
    layer_out = mixed.reshape(rows * steps, width) + routed
    return layer_out.astype(jnp.bfloat16).reshape(rows, steps, width)


VMEM = pl.BlockSpec(memory_space=pltpu.VMEM)
SMEM = pl.BlockSpec(memory_space=pltpu.SMEM)
LANES = 128
VMEM_BYTES = 34 * 2**20
MAIN = 8


def stack(parts, axis=0):
    return jnp.concatenate(parts, axis=axis)


def front_kernel(
    q_ref, nk_ref, nv_ref, ck_ref, cv_ref, len_ref, grid_ref, res_ref, gain_ref, routes_ref,
    gains_ref, pay_ref, mixed_ref,
):
    rows, steps, width = q_ref.shape
    ctx = ck_ref.shape[1]
    kv_count = ck_ref.shape[2] // HEAD_DIM
    group = width // HEAD_DIM // kv_count
    half = HEAD_DIM // 2
    tall = group * steps
    fresh_pad = 8
    keys = ctx + fresh_pad
    lane = lax.broadcasted_iota(jnp.int32, (8, HEAD_DIM), 1)
    freq = jnp.exp((lane % half).astype(jnp.float32) * (-2.0 * math.log(THETA) / HEAD_DIM))
    sub = lax.broadcasted_iota(jnp.int32, (8, HEAD_DIM), 0)
    flip = jnp.where(lane < half, -1.0, 1.0)
    head_step = lax.broadcasted_iota(jnp.int32, (tall, keys), 0) % steps
    column = lax.broadcasted_iota(jnp.int32, (tall, keys), 1)
    fresh_live = (column >= ctx) & (column - ctx <= head_step)
    scale = 1.0 / math.sqrt(HEAD_DIM)

    def turn(vectors, cosine, sine):
        return vectors * cosine + pltpu.roll(vectors, half, 1) * sine

    gain = gain_ref[...].astype(jnp.float32).reshape(1, width)
    normed = []
    for r in range(rows):
        length = len_ref[r]
        high, wide = grid_ref[0, r], grid_ref[1, r]
        base = length - high * wide + jnp.maximum(high, wide)
        angle = (base + sub % steps).astype(jnp.float32) * freq
        cosine = jnp.cos(angle)
        sine = jnp.sin(angle) * flip
        cosines = stack([cosine] * (tall // 8))
        sines = stack([sine] * (tall // 8))
        live = (column < jnp.minimum(length, ctx)) | fresh_live
        q_r = q_ref[r].astype(jnp.float32)
        nk_r = nk_ref[r].astype(jnp.float32)
        nv_r = nv_ref[r].astype(jnp.float32)
        ck_r = ck_ref[r].astype(jnp.float32)
        cv_r = cv_ref[r].astype(jnp.float32)
        blank = jnp.zeros((fresh_pad - steps, HEAD_DIM), jnp.float32)
        pieces = []
        for g in range(kv_count):
            cols = slice(g * HEAD_DIM, (g + 1) * HEAD_DIM)
            first = g * group
            query = stack(
                [q_r[:, (first + h) * HEAD_DIM : (first + h + 1) * HEAD_DIM] for h in range(group)]
            )
            query = turn(query, cosines, sines)
            fresh = turn(stack([nk_r[:, cols], blank]), cosine, sine)
            key = stack([ck_r[:, cols], fresh])
            scores = (
                lax.dot_general(
                    query, key, (((1,), (1,)), ((), ())),
                    precision=lax.Precision.HIGHEST, preferred_element_type=jnp.float32,
                )
                * scale
            )
            scores = jnp.where(live, scores, MASKED)
            top = jnp.max(scores, axis=-1, keepdims=True)
            weights = jnp.exp(scores - top)
            probs = (weights / jnp.sum(weights, axis=-1, keepdims=True)).astype(jnp.bfloat16)
            value = stack([cv_r[:, cols], nv_r[:, cols], blank]).astype(jnp.bfloat16)
            out = jnp.dot(probs, value, preferred_element_type=jnp.float32)
            out = out.astype(jnp.bfloat16).astype(jnp.float32)
            pieces += [out[h * steps : (h + 1) * steps] for h in range(group)]
        mixed = res_ref[r].astype(jnp.float32) + stack(pieces, axis=1)
        mixed_ref[r] = mixed
        mean = jnp.mean(mixed * mixed, axis=-1, keepdims=True)
        normed.append(mixed * lax.rsqrt(mean + EPS) * gain)

    whole = MAIN // steps
    fold = width // 2
    pay_ref[:, :width] = stack(normed[:whole]).astype(pay_ref.dtype)
    late = normed[whole:]
    pay_ref[:, width : width + fold] = stack(
        [n[:, :fold] for n in late] + [n[:, fold:] for n in late]
    ).astype(pay_ref.dtype)

    place = lax.broadcasted_iota(jnp.int32, (steps, LANES), 1)
    spread = []
    for r in range(rows):
        gains = gains_ref[r]
        shares = gains / jnp.sum(gains, axis=-1, keepdims=True)
        picks = routes_ref[r] + (0 if r < whole else LANES // 2)
        dense = jnp.zeros((steps, LANES), jnp.float32)
        for k in range(TOP):
            dense = jnp.where(place == picks[:, k : k + 1], shares[:, k : k + 1], dense)
        spread.append(dense)
    early = stack(spread[:whole])
    late = stack(spread[whole:] + [jnp.zeros((MAIN - (rows - whole) * steps, LANES), jnp.float32)])
    pay_ref[:, width + fold :] = (early + late).astype(pay_ref.dtype)


def front(queries, new_keys, new_values, cache_keys, cache_values, lengths, image_grid, residual,
          norm_gain, routes, route_gains):
    rows, steps, width = queries.shape
    return pl.pallas_call(
        front_kernel,
        out_shape=(
            jax.ShapeDtypeStruct((MAIN, width + width // 2 + LANES), jnp.bfloat16),
            jax.ShapeDtypeStruct((rows, steps, width), jnp.float32),
        ),
        in_specs=[VMEM] * 5 + [SMEM] * 2 + [VMEM] * 4,
        out_specs=(VMEM, VMEM),
        cost_estimate=pl.CostEstimate(flops=10**7, bytes_accessed=10**6, transcendentals=10**4),
    )(queries, new_keys, new_values, cache_keys, cache_values, lengths, image_grid.T, residual,
      norm_gain, routes, route_gains)


GROUP = 4
CUT = 256


def fetch_kernel(parts, *refs):
    sources, (_, *outs, sem) = refs[:parts], refs[parts:]
    copies = [
        pltpu.make_async_copy(source.at[e], out.at[e], sem.at[p, e])
        for p, (source, out) in enumerate(zip(sources, outs))
        for e in range(out.shape[0])
    ]
    for copy in copies:
        copy.start()
    for copy in copies:
        copy.wait()


def fetch(weights, count, after):
    size = weights[0].size * 2 // weights[0].shape[0] * count * len(weights)
    place = pl.BlockSpec(memory_space=pl.ANY)
    shape = (count, *weights[0].shape[1:])
    return pl.pallas_call(
        functools.partial(fetch_kernel, len(weights)),
        out_shape=[pltpu.VMEM(shape, jnp.bfloat16)] * len(weights),
        in_specs=[place] * (len(weights) + 1),
        out_specs=[VMEM] * len(weights),
        scratch_shapes=[pltpu.SemaphoreType.DMA((len(weights), count))],
        compiler_params=pltpu.CompilerParams(vmem_limit_bytes=2**20),
        cost_estimate=pl.CostEstimate(flops=0, bytes_accessed=size, transcendentals=0),
    )(*[pltpu.with_memory_space_constraint(w, pltpu.HBM) for w in weights], after)


def experts_kernel(blocks, axis, *refs):
    pays = refs[:blocks]
    (
        early_gate, early_up, early_down, gate_hbm, up_hbm, down_hbm, near_ref, far_ref, held_ref,
        x_ref, share_ref, hidden_ref, held_sem,
    ) = refs[blocks:]
    local, quarter, width = gate_hbm.shape
    fold = width // 2
    rest = 4
    tokens = blocks * (MAIN + rest)
    tall = GROUP * quarter
    groups = local // GROUP
    half = local // 2

    def load(g):
        slot = g % 2
        copies = []
        for k in range(GROUP):
            if g < groups:
                e = g * GROUP + k
                pair = gate_hbm.at[e], up_hbm.at[e]
            else:
                pair = down_hbm.at[half + k], down_hbm.at[half + GROUP + k]
            for p in range(2):
                copies.append(
                    pltpu.make_async_copy(
                        pair[p], held_ref.at[slot, p, k], held_sem.at[slot, p, k]
                    )
                )
        return copies

    for g in (1, 2):
        for copy in load(g):
            copy.start()

    spread = []
    for i in range(0, blocks, 2):
        pair = [pays[i + j][...].astype(jnp.float32) for j in range(2)]
        x_ref[i * MAIN : (i + 2) * MAIN] = stack([p[:, :width] for p in pair]).astype(x_ref.dtype)
        spread += [p[:, width + fold :] for p in pair]
    for i in range(0, blocks, 4):
        start = blocks * MAIN + i * rest
        four = [pays[i + j][...].astype(jnp.float32) for j in range(4)]
        left = stack([p[:rest, width : width + fold] for p in four])
        right = stack([p[rest:, width : width + fold] for p in four])
        x_ref[start : start + 4 * rest, :fold] = left.astype(x_ref.dtype)
        x_ref[start : start + 4 * rest, fold:] = right.astype(x_ref.dtype)
        spread += [p[:rest, width + fold :] for p in four]
    shares = stack(spread).T
    column = lax.broadcasted_iota(jnp.int32, (LANES // 2, tokens), 1)
    share_ref[...] = jnp.where(
        column < blocks * MAIN, shares[: LANES // 2], shares[LANES // 2 :]
    )
    first = lax.axis_index(axis) * local

    for g in range(groups):
        if g == 0:
            gate_w, up_w = early_gate[...], early_up[...]
        else:
            for copy in load(g):
                copy.wait()
            gate_w, up_w = held_ref[g % 2, 0], held_ref[g % 2, 1]
        flat = (((1,), (1,)), ((), ()))
        gate = lax.dot_general(
            gate_w.reshape(tall, width), x_ref[...], flat, preferred_element_type=jnp.float32
        )
        upper = lax.dot_general(
            up_w.reshape(tall, width), x_ref[...], flat, preferred_element_type=jnp.float32
        )
        hidden = jax.nn.silu(gate) * upper
        weight = stack(
            [
                jnp.broadcast_to(share_ref[pl.ds(first + g * GROUP + k, 1)], (quarter, tokens))
                for k in range(GROUP)
            ]
        )
        hidden_ref[:, g * tall : (g + 1) * tall] = (hidden * weight).T.astype(hidden_ref.dtype)
        if 1 <= g < groups - 1:
            for copy in load(g + 2):
                copy.start()

    for copy in load(groups):
        copy.wait()
    deep = half * quarter
    slot = groups % 2
    for at in range(0, fold, CUT):
        low, high = [
            jnp.dot(
                hidden_ref[:, :deep], early_down[:, :, c : c + CUT].reshape(deep, CUT),
                preferred_element_type=jnp.float32,
            )
            + jnp.dot(
                hidden_ref[:, deep:], held_ref[slot, :, :, :, c : c + CUT].reshape(deep, CUT),
                preferred_element_type=jnp.float32,
            )
            for c in (at, fold + at)
        ]
        for b in range(blocks):
            out = near_ref if b < blocks // 2 else far_ref
            to = b % (blocks // 2)
            main = slice(b * MAIN, (b + 1) * MAIN)
            out[to, :, at : at + CUT] = low[main].astype(out.dtype)
            out[to, :, fold + at : fold + at + CUT] = high[main].astype(out.dtype)
            start = blocks * MAIN + b * rest
            late = stack([low[start : start + rest], high[start : start + rest]])
            out[to, :, width + at : width + at + CUT] = late.astype(out.dtype)


def experts(pays, early, w_gate, w_up, w_down, axis):
    blocks = len(pays)
    local, quarter, width = w_down.shape
    tokens = blocks * 12
    packed = width + width // 2
    half = jax.ShapeDtypeStruct((blocks // 2, MAIN, packed), jnp.bfloat16)
    place = pl.BlockSpec(memory_space=pl.ANY)
    held = [pltpu.with_memory_space_constraint(a, pltpu.VMEM) for a in (*pays, *early)]
    return pl.pallas_call(
        functools.partial(experts_kernel, blocks, axis),
        out_shape=(half, half),
        in_specs=[VMEM] * len(held) + [place] * 3,
        out_specs=(VMEM, VMEM),
        scratch_shapes=[
            pltpu.VMEM((2, 2, GROUP, quarter, width), jnp.bfloat16),
            pltpu.VMEM((tokens, width), jnp.bfloat16),
            pltpu.VMEM((LANES // 2, tokens), jnp.float32),
            pltpu.VMEM((tokens, local * quarter), jnp.bfloat16),
            pltpu.SemaphoreType.DMA((2, 2, GROUP)),
        ],
        compiler_params=pltpu.CompilerParams(vmem_limit_bytes=VMEM_BYTES),
        cost_estimate=pl.CostEstimate(
            flops=6 * tokens * local * quarter * width,
            bytes_accessed=4 * local * quarter * width,
            transcendentals=tokens * local * quarter,
        ),
    )(*held, *[pltpu.with_memory_space_constraint(w, pltpu.HBM) for w in (w_gate, w_up, w_down)])


def final_kernel(mixed_ref, *refs):
    parts, out_ref = refs[:-1], refs[-1]
    rows, steps, width = mixed_ref.shape
    fold = width // 2
    total = parts[0][...].astype(jnp.float32)
    for part in parts[1:]:
        total = total + part[...].astype(jnp.float32)
    for r in range(rows):
        at = r * steps
        if at < MAIN:
            routed = total[at : at + steps, :width]
        else:
            at -= MAIN
            low = total[at : at + steps, width:]
            at += MAIN // 2
            routed = stack([low, total[at : at + steps, width:]], axis=1)
        out_ref[r] = (mixed_ref[r] + routed).astype(out_ref.dtype)


def gathered(
    queries, new_keys, new_values, cache_keys, cache_values, lengths, image_grid, residual,
    norm_gain, routes, route_gains, w_gate, w_up, w_down,
):
    members = lax.axis_size("expert")
    pay, mixed = front(
        queries, new_keys, new_values, cache_keys, cache_values, lengths, image_grid, residual,
        norm_gain, routes, route_gains,
    )
    twin = [(0, 1), (1, 0), (2, 3), (3, 2)]
    side = [(0, 2), (2, 0), (1, 3), (3, 1)]
    shifts = (2, 1, 3)
    ahead = {k: [(i, (i + k) % members) for i in range(members)] for k in shifts}
    back = {k: [(i, (i - k) % members) for i in range(members)] for k in shifts}
    line = [pay] + [lax.ppermute(pay, "expert", ahead[k]) for k in shifts]
    gate, up = jnp.swapaxes(w_gate, 1, 2), jnp.swapaxes(w_up, 1, 2)
    pair = fetch((gate, up), GROUP, pay)
    line[1], *pair = lax.optimization_barrier((line[1], *pair))
    pays = line + [lax.ppermute(p, "dp", side) for p in line]
    (down,) = fetch((w_down,), w_down.shape[0] // 2, line[-1])
    pays[5], down = lax.optimization_barrier((pays[5], down))
    pays = pays + [lax.ppermute(p, "dp", twin) for p in pays]
    near, far = experts(pays, (*pair, down), gate, up, w_down, "expert")
    far = lax.ppermute(far, "dp", twin)
    near = (near.astype(jnp.float32) + far.astype(jnp.float32)).astype(jnp.bfloat16)
    peer = lax.ppermute(near[members:], "dp", side)
    near = (near[:members].astype(jnp.float32) + peer.astype(jnp.float32)).astype(jnp.bfloat16)
    parts = [near[0]] + [
        lax.ppermute(near[i + 1], "expert", back[k]) for i, k in enumerate(shifts)
    ]
    return pl.pallas_call(
        final_kernel,
        out_shape=jax.ShapeDtypeStruct(residual.shape, jnp.bfloat16),
        in_specs=[VMEM] * (1 + members),
        out_specs=VMEM,
    )(mixed, *parts)


def solution(mesh):
    placed = (
        P(("replica", "expert", "dp"), None, None),
        P(("replica", "expert", "dp"), None, None),
        P(("replica", "expert", "dp"), None, None),
        P(("replica", "expert", "dp"), None, None),
        P(("replica", "expert", "dp"), None, None),
        P(("replica", "expert", "dp")),
        P(("replica", "expert", "dp"), None),
        P(("replica", "expert", "dp"), None, None),
        P(),
        P(("replica", "expert", "dp"), None, None),
        P(("replica", "expert", "dp"), None, None),
        P("expert", None, "dp"),
        P("expert", None, "dp"),
        P("expert", "dp", None),
    )
    near = mesh.shape["expert"] == 4 and mesh.shape["dp"] == 4
    return jax.shard_map(
        gathered if near else shards,
        mesh=mesh,
        in_specs=placed,
        out_specs=P(("replica", "expert", "dp"), None, None),
        check_vma=False,
    )
```

```python
import functools
import math

import jax
import jax.numpy as jnp
from jax import lax
from jax.experimental import pallas as pl
from jax.experimental.pallas import tpu as pltpu
from jax.sharding import PartitionSpec as P

HEAD_DIM = 128
TOP = 8
CAP = 2


THETA = 5000000.0
EPS = 1e-06
MASKED = -1e30


def rotate(vectors, where):
    half = vectors.shape[-1] // 2
    freq = THETA ** (-2.0 * jnp.arange(half, dtype=jnp.float32) / vectors.shape[-1])
    angle = where[..., None] * freq
    cosine = jnp.cos(angle)
    sine = jnp.sin(angle)
    first = vectors[..., :half]
    second = vectors[..., half:]
    return jnp.concatenate(
        [first * cosine - second * sine, second * cosine + first * sine], axis=-1
    )


def attend(queries, new_keys, new_values, cache_keys, cache_values, lengths, image_grid):
    count = queries.shape[0]
    steps = queries.shape[1]
    ctx = cache_keys.shape[1]
    kv_count = cache_keys.shape[2] // HEAD_DIM
    group = queries.shape[2] // HEAD_DIM // kv_count
    base = (
        lengths
        - image_grid[:, 0] * image_grid[:, 1]
        + jnp.maximum(image_grid[:, 0], image_grid[:, 1])
    )
    where = (base[:, None] + jnp.arange(steps, dtype=jnp.int32)[None, :]).astype(jnp.float32)
    query = rotate(
        queries.astype(jnp.float32).reshape(count, steps, kv_count, group, HEAD_DIM),
        where[:, :, None, None],
    )
    fresh = rotate(
        new_keys.astype(jnp.float32).reshape(count, steps, kv_count, HEAD_DIM), where[:, :, None]
    )
    cached = cache_keys.astype(jnp.float32).reshape(count, ctx, kv_count, HEAD_DIM)
    scale = 1.0 / math.sqrt(HEAD_DIM)
    old_scores = (
        jnp.einsum("rsgqd,rcgd->rsgqc", query, cached, precision=lax.Precision.HIGHEST) * scale
    )
    new_scores = (
        jnp.einsum("rsgqd,rtgd->rsgqt", query, fresh, precision=lax.Precision.HIGHEST) * scale
    )
    live = jnp.arange(ctx, dtype=jnp.int32)[None, :] < lengths[:, None]
    old_scores = jnp.where(live[:, None, None, None, :], old_scores, MASKED)
    causal = (
        jnp.arange(steps, dtype=jnp.int32)[None, :] <= jnp.arange(steps, dtype=jnp.int32)[:, None]
    )
    new_scores = jnp.where(causal[None, :, None, None, :], new_scores, MASKED)
    scores = jnp.concatenate([old_scores, new_scores], axis=-1)
    top = jnp.max(scores, axis=-1, keepdims=True)
    weights = jnp.exp(scores - top)
    probs = (weights / jnp.sum(weights, axis=-1, keepdims=True)).astype(jnp.bfloat16)
    values = jnp.concatenate(
        [
            cache_values.reshape(count, ctx, kv_count, HEAD_DIM),
            new_values.reshape(count, steps, kv_count, HEAD_DIM),
        ],
        axis=1,
    )
    out = jnp.einsum("rsgqc,rcgd->rsgqd", probs, values, preferred_element_type=jnp.float32)
    return out.astype(jnp.bfloat16).reshape(count, steps, -1)


def shards(
    queries,
    new_keys,
    new_values,
    cache_keys,
    cache_values,
    lengths,
    image_grid,
    residual,
    norm_gain,
    routes,
    route_gains,
    w_gate,
    w_up,
    w_down,
):
    rows, steps, width = residual.shape
    attended = attend(queries, new_keys, new_values, cache_keys, cache_values, lengths, image_grid)
    mixed = residual.astype(jnp.float32) + attended.astype(jnp.float32)
    normed = (
        mixed
        * lax.rsqrt(jnp.mean(mixed * mixed, axis=-1, keepdims=True) + EPS)
        * norm_gain.astype(jnp.float32)
    ).astype(jnp.bfloat16)
    shares = (route_gains / jnp.sum(route_gains, axis=-1, keepdims=True)).astype(jnp.bfloat16)
    members = lax.axis_size("expert")
    local = w_gate.shape[0]
    places = members * CAP * local
    picks = routes.reshape(-1)
    onehot = (picks[:, None] == jnp.arange(members * local, dtype=jnp.int32)[None, :]).astype(
        jnp.int32
    )
    earlier = jnp.sum((jnp.cumsum(onehot, axis=0) - onehot) * onehot, axis=1)
    target = picks // local * (CAP * local) + earlier * local + picks % local
    placed = (target[:, None] == jnp.arange(places, dtype=jnp.int32)[None, :]).reshape(
        rows * steps, TOP, places
    )
    chooser = jnp.sum(placed.astype(jnp.float32), axis=1).astype(jnp.bfloat16)
    weigher = jnp.sum(
        jnp.where(
            placed, shares.reshape(rows * steps, TOP, 1).astype(jnp.float32), jnp.float32(0.0)
        ),
        axis=1,
    ).astype(jnp.bfloat16)
    outgoing = jnp.einsum(
        "jp,jd->pd",
        chooser,
        normed.reshape(rows * steps, width),
        preferred_element_type=jnp.float32,
    )
    outgoing = outgoing.astype(jnp.bfloat16).reshape(members, CAP, local, width)
    incoming = lax.all_to_all(outgoing, "expert", split_axis=0, concat_axis=0, tiled=True)
    flat = incoming.reshape(-1, local, width)
    piece = lax.all_gather(flat, "dp", axis=0, tiled=True)
    gate = jnp.einsum("red,edh->reh", piece, w_gate, preferred_element_type=jnp.float32)
    upper = jnp.einsum("red,edh->reh", piece, w_up, preferred_element_type=jnp.float32)
    hidden = (jax.nn.silu(gate) * upper).astype(jnp.bfloat16)
    piece = hidden
    result = lax.psum_scatter(
        jnp.einsum("reh,ehd->red", piece, w_down, preferred_element_type=jnp.float32).astype(
            jnp.bfloat16
        ),
        "dp",
        scatter_dimension=0,
        tiled=True,
    )
    returned = lax.all_to_all(
        result.reshape(incoming.shape), "expert", split_axis=0, concat_axis=0, tiled=True
    )
    routed = jnp.dot(weigher, returned.reshape(places, width), preferred_element_type=jnp.float32)
    layer_out = mixed.reshape(rows * steps, width) + routed
    return layer_out.astype(jnp.bfloat16).reshape(rows, steps, width)


VMEM = pl.BlockSpec(memory_space=pltpu.VMEM)
SMEM = pl.BlockSpec(memory_space=pltpu.SMEM)
LANES = 128
VMEM_BYTES = 34 * 2**20
MAIN = 8


def stack(parts, axis=0):
    return jnp.concatenate(parts, axis=axis)


def front_kernel(
    q_ref, nk_ref, nv_ref, ck_ref, cv_ref, len_ref, grid_ref, res_ref, gain_ref, routes_ref,
    gains_ref, pay_ref, mixed_ref,
):
    rows, steps, width = q_ref.shape
    ctx = ck_ref.shape[1]
    kv_count = ck_ref.shape[2] // HEAD_DIM
    group = width // HEAD_DIM // kv_count
    half = HEAD_DIM // 2
    tall = group * steps
    fresh_pad = 8
    keys = ctx + fresh_pad
    lane = lax.broadcasted_iota(jnp.int32, (8, HEAD_DIM), 1)
    freq = jnp.exp((lane % half).astype(jnp.float32) * (-2.0 * math.log(THETA) / HEAD_DIM))
    sub = lax.broadcasted_iota(jnp.int32, (8, HEAD_DIM), 0)
    flip = jnp.where(lane < half, -1.0, 1.0)
    head_step = lax.broadcasted_iota(jnp.int32, (tall, keys), 0) % steps
    column = lax.broadcasted_iota(jnp.int32, (tall, keys), 1)
    fresh_live = (column >= ctx) & (column - ctx <= head_step)
    scale = 1.0 / math.sqrt(HEAD_DIM)

    def turn(vectors, cosine, sine):
        return vectors * cosine + pltpu.roll(vectors, half, 1) * sine

    gain = gain_ref[...].astype(jnp.float32).reshape(1, width)
    normed = []
    for r in range(rows):
        length = len_ref[r]
        high, wide = grid_ref[0, r], grid_ref[1, r]
        base = length - high * wide + jnp.maximum(high, wide)
        angle = (base + sub % steps).astype(jnp.float32) * freq
        cosine = jnp.cos(angle)
        sine = jnp.sin(angle) * flip
        cosines = stack([cosine] * (tall // 8))
        sines = stack([sine] * (tall // 8))
        live = (column < jnp.minimum(length, ctx)) | fresh_live
        q_r = q_ref[r].astype(jnp.float32)
        nk_r = nk_ref[r].astype(jnp.float32)
        nv_r = nv_ref[r].astype(jnp.float32)
        ck_r = ck_ref[r].astype(jnp.float32)
        cv_r = cv_ref[r].astype(jnp.float32)
        blank = jnp.zeros((fresh_pad - steps, HEAD_DIM), jnp.float32)
        pieces = []
        for g in range(kv_count):
            cols = slice(g * HEAD_DIM, (g + 1) * HEAD_DIM)
            first = g * group
            query = stack(
                [q_r[:, (first + h) * HEAD_DIM : (first + h + 1) * HEAD_DIM] for h in range(group)]
            )
            query = turn(query, cosines, sines)
            fresh = turn(stack([nk_r[:, cols], blank]), cosine, sine)
            key = stack([ck_r[:, cols], fresh])
            scores = (
                lax.dot_general(
                    query, key, (((1,), (1,)), ((), ())),
                    precision=lax.Precision.HIGHEST, preferred_element_type=jnp.float32,
                )
                * scale
            )
            scores = jnp.where(live, scores, MASKED)
            top = jnp.max(scores, axis=-1, keepdims=True)
            weights = jnp.exp(scores - top)
            probs = (weights / jnp.sum(weights, axis=-1, keepdims=True)).astype(jnp.bfloat16)
            value = stack([cv_r[:, cols], nv_r[:, cols], blank]).astype(jnp.bfloat16)
            out = jnp.dot(probs, value, preferred_element_type=jnp.float32)
            out = out.astype(jnp.bfloat16).astype(jnp.float32)
            pieces += [out[h * steps : (h + 1) * steps] for h in range(group)]
        mixed = res_ref[r].astype(jnp.float32) + stack(pieces, axis=1)
        mixed_ref[r] = mixed
        mean = jnp.mean(mixed * mixed, axis=-1, keepdims=True)
        normed.append(mixed * lax.rsqrt(mean + EPS) * gain)

    whole = MAIN // steps
    fold = width // 2
    pay_ref[:, :width] = stack(normed[:whole]).astype(pay_ref.dtype)
    late = normed[whole:]
    pay_ref[:, width : width + fold] = stack(
        [n[:, :fold] for n in late] + [n[:, fold:] for n in late]
    ).astype(pay_ref.dtype)

    place = lax.broadcasted_iota(jnp.int32, (steps, LANES), 1)
    spread = []
    for r in range(rows):
        gains = gains_ref[r]
        shares = gains / jnp.sum(gains, axis=-1, keepdims=True)
        picks = routes_ref[r] + (0 if r < whole else LANES // 2)
        dense = jnp.zeros((steps, LANES), jnp.float32)
        for k in range(TOP):
            dense = jnp.where(place == picks[:, k : k + 1], shares[:, k : k + 1], dense)
        spread.append(dense)
    early = stack(spread[:whole])
    late = stack(spread[whole:] + [jnp.zeros((MAIN - (rows - whole) * steps, LANES), jnp.float32)])
    pay_ref[:, width + fold :] = (early + late).astype(pay_ref.dtype)


def front(queries, new_keys, new_values, cache_keys, cache_values, lengths, image_grid, residual,
          norm_gain, routes, route_gains):
    rows, steps, width = queries.shape
    return pl.pallas_call(
        front_kernel,
        out_shape=(
            jax.ShapeDtypeStruct((MAIN, width + width // 2 + LANES), jnp.bfloat16),
            jax.ShapeDtypeStruct((rows, steps, width), jnp.float32),
        ),
        in_specs=[VMEM] * 5 + [SMEM] * 2 + [VMEM] * 4,
        out_specs=(VMEM, VMEM),
        cost_estimate=pl.CostEstimate(flops=10**7, bytes_accessed=10**6, transcendentals=10**4),
    )(queries, new_keys, new_values, cache_keys, cache_values, lengths, image_grid.T, residual,
      norm_gain, routes, route_gains)


GROUP = 4
CUT = 512


def fetch_kernel(parts, start, *refs):
    sources, (_, *outs, sem) = refs[:parts], refs[parts:]
    copies = [
        pltpu.make_async_copy(source.at[start + e], out.at[e], sem.at[p, e])
        for p, (source, out) in enumerate(zip(sources, outs))
        for e in range(out.shape[0])
    ]
    for copy in copies:
        copy.start()
    for copy in copies:
        copy.wait()


def fetch(weights, start, count, after):
    size = weights[0].size * 2 // weights[0].shape[0] * count * len(weights)
    place = pl.BlockSpec(memory_space=pl.ANY)
    shape = (count, *weights[0].shape[1:])
    return pl.pallas_call(
        functools.partial(fetch_kernel, len(weights), start),
        out_shape=[pltpu.VMEM(shape, jnp.bfloat16)] * len(weights),
        in_specs=[place] * (len(weights) + 1),
        out_specs=[VMEM] * len(weights),
        scratch_shapes=[pltpu.SemaphoreType.DMA((len(weights), count))],
        compiler_params=pltpu.CompilerParams(vmem_limit_bytes=2**20),
        cost_estimate=pl.CostEstimate(flops=0, bytes_accessed=size, transcendentals=0),
    )(*[pltpu.with_memory_space_constraint(w, pltpu.HBM) for w in weights], after)


def experts_kernel(blocks, axis, *refs):
    pays = refs[:blocks]
    (
        _, _, _, _, gate_hbm, up_hbm, down_hbm, near_ref, far_ref, gate_a, up_a, gate_b, up_b,
        held_ref, x_ref, share_ref, hidden_ref, held_sem, down_sem,
    ) = refs[blocks:]
    early = (gate_a, up_a, gate_b, up_b)
    local, quarter, width = gate_hbm.shape
    fold = width // 2
    rest = 4
    tokens = blocks * (MAIN + rest)
    tall = GROUP * quarter
    groups = local // GROUP
    ready = len(early) // 2

    def load(g):
        return [
            pltpu.make_async_copy(
                source.at[g * GROUP + k], held_ref.at[g - ready, p, k], held_sem.at[g - ready, p, k]
            )
            for p, source in enumerate((gate_hbm, up_hbm))
            for k in range(GROUP)
        ]

    cuts = fold // CUT

    def load_down(c):
        return [
            pltpu.make_async_copy(
                down_hbm.at[pl.ds(q * GROUP, GROUP), :, pl.ds(side * fold + c * CUT, CUT)],
                early[q].at[:, :, pl.ds(side * fold + c * CUT, CUT)],
                down_sem.at[c, q, side],
            )
            for q in range(groups)
            for side in range(2)
        ]

    for g in range(ready, groups):
        for copy in load(g):
            copy.start()

    spread = []
    for i in range(0, blocks, 2):
        pair = [pays[i + j][...].astype(jnp.float32) for j in range(2)]
        x_ref[i * MAIN : (i + 2) * MAIN] = stack([p[:, :width] for p in pair]).astype(x_ref.dtype)
        spread += [p[:, width + fold :] for p in pair]
    for i in range(0, blocks, 4):
        start = blocks * MAIN + i * rest
        four = [pays[i + j][...].astype(jnp.float32) for j in range(4)]
        left = stack([p[:rest, width : width + fold] for p in four])
        right = stack([p[rest:, width : width + fold] for p in four])
        x_ref[start : start + 4 * rest, :fold] = left.astype(x_ref.dtype)
        x_ref[start : start + 4 * rest, fold:] = right.astype(x_ref.dtype)
        spread += [p[:rest, width + fold :] for p in four]
    shares = stack(spread).T
    column = lax.broadcasted_iota(jnp.int32, (LANES // 2, tokens), 1)
    share_ref[...] = jnp.where(
        column < blocks * MAIN, shares[: LANES // 2], shares[LANES // 2 :]
    )
    first = lax.axis_index(axis) * local

    flat = (((1,), (1,)), ((), ()))

    def finish(g, gate, upper):
        hidden = jax.nn.silu(gate) * upper
        weight = stack(
            [
                jnp.broadcast_to(share_ref[pl.ds(first + g * GROUP + k, 1)], (quarter, tokens))
                for k in range(GROUP)
            ]
        )
        hidden_ref[:, g * tall : (g + 1) * tall] = (hidden * weight).T.astype(hidden_ref.dtype)

    made = None
    for g in range(groups):
        if g >= ready:
            for copy in load(g):
                copy.wait()
            few = -(-cuts // (groups - ready))
            for c in range((g - ready) * few, min((g - ready + 1) * few, cuts)):
                for copy in load_down(c):
                    copy.start()
        if g < ready:
            gate_at, up_at = early[2 * g], early[2 * g + 1]
        else:
            gate_at, up_at = held_ref.at[g - ready, 0], held_ref.at[g - ready, 1]
        gate, upper = [
            lax.dot_general(
                at[...].reshape(tall, width), x_ref[...], flat, preferred_element_type=jnp.float32
            )
            for at in (gate_at, up_at)
        ]
        if made is not None:
            finish(g - 1, *made)
        made = gate, upper
    for c in range(cuts):
        at = c * CUT
        for copy in load_down(c):
            copy.wait()
        if c == 0:
            finish(groups - 1, *made)
        low, high = [
            sum(
                jnp.dot(
                    hidden_ref[:, q * tall : (q + 1) * tall],
                    early[q][:, :, c : c + CUT].reshape(tall, CUT),
                    preferred_element_type=jnp.float32,
                )
                for q in range(groups)
            )
            for c in (at, fold + at)
        ]
        for b in range(blocks):
            out = near_ref if b < blocks // 2 else far_ref
            to = b % (blocks // 2)
            main = slice(b * MAIN, (b + 1) * MAIN)
            out[to, :, at : at + CUT] = low[main].astype(out.dtype)
            out[to, :, fold + at : fold + at + CUT] = high[main].astype(out.dtype)
            start = blocks * MAIN + b * rest
            late = stack([low[start : start + rest], high[start : start + rest]])
            out[to, :, width + at : width + at + CUT] = late.astype(out.dtype)


def experts(pays, early, w_gate, w_up, w_down, axis):
    blocks = len(pays)
    local, quarter, width = w_down.shape
    tokens = blocks * 12
    packed = width + width // 2
    half = jax.ShapeDtypeStruct((blocks // 2, MAIN, packed), jnp.bfloat16)
    place = pl.BlockSpec(memory_space=pl.ANY)
    held = [pltpu.with_memory_space_constraint(a, pltpu.VMEM) for a in (*pays, *early)]
    return pl.pallas_call(
        functools.partial(experts_kernel, blocks, axis),
        out_shape=[half, half] + [pltpu.VMEM(a.shape, a.dtype) for a in early],
        in_specs=[VMEM] * len(held) + [place] * 3,
        out_specs=[VMEM] * (2 + len(early)),
        input_output_aliases={blocks + i: 2 + i for i in range(len(early))},
        scratch_shapes=[
            pltpu.VMEM((local // GROUP - 2, 2, GROUP, quarter, width), jnp.bfloat16),
            pltpu.VMEM((tokens, width), jnp.bfloat16),
            pltpu.VMEM((LANES // 2, tokens), jnp.float32),
            pltpu.VMEM((tokens, local * quarter), jnp.bfloat16),
            pltpu.SemaphoreType.DMA((local // GROUP - 2, 2, GROUP)),
            pltpu.SemaphoreType.DMA((width // 2 // CUT, local // GROUP, 2)),
        ],
        compiler_params=pltpu.CompilerParams(vmem_limit_bytes=VMEM_BYTES),
        cost_estimate=pl.CostEstimate(
            flops=6 * tokens * local * quarter * width,
            bytes_accessed=4 * local * quarter * width,
            transcendentals=tokens * local * quarter,
        ),
    )(*held, *[pltpu.with_memory_space_constraint(w, pltpu.HBM) for w in (w_gate, w_up, w_down)])[:2]


def final_kernel(mixed_ref, *refs):
    parts, out_ref = refs[:-1], refs[-1]
    rows, steps, width = mixed_ref.shape
    fold = width // 2
    total = parts[0][...].astype(jnp.float32)
    for part in parts[1:]:
        total = total + part[...].astype(jnp.float32)
    for r in range(rows):
        at = r * steps
        if at < MAIN:
            routed = total[at : at + steps, :width]
        else:
            at -= MAIN
            low = total[at : at + steps, width:]
            at += MAIN // 2
            routed = stack([low, total[at : at + steps, width:]], axis=1)
        out_ref[r] = (mixed_ref[r] + routed).astype(out_ref.dtype)


def gathered(
    queries, new_keys, new_values, cache_keys, cache_values, lengths, image_grid, residual,
    norm_gain, routes, route_gains, w_gate, w_up, w_down,
):
    members = lax.axis_size("expert")
    pay, mixed = front(
        queries, new_keys, new_values, cache_keys, cache_values, lengths, image_grid, residual,
        norm_gain, routes, route_gains,
    )
    twin = [(0, 1), (1, 0), (2, 3), (3, 2)]
    side = [(0, 2), (2, 0), (1, 3), (3, 1)]
    shifts = (2, 1, 3)
    ahead = {k: [(i, (i + k) % members) for i in range(members)] for k in shifts}
    back = {k: [(i, (i - k) % members) for i in range(members)] for k in shifts}
    line = [pay] + [lax.ppermute(pay, "expert", ahead[k]) for k in shifts]
    gate, up = jnp.swapaxes(w_gate, 1, 2), jnp.swapaxes(w_up, 1, 2)
    pair = fetch((gate, up), 0, GROUP, pay)
    line[1], *pair = lax.optimization_barrier((line[1], *pair))
    pays = line + [lax.ppermute(p, "dp", side) for p in line]
    second = fetch((gate, up), GROUP, GROUP, line[-1])
    *x_side, first_two, next_two = lax.optimization_barrier((*pays[members:], *second))
    second = [first_two, next_two]
    pays = pays[:members] + x_side
    pays = pays + [lax.ppermute(p, "dp", twin) for p in pays]
    near, far = experts(pays, (*pair, *second), gate, up, w_down, "expert")
    far = lax.ppermute(far, "dp", twin)
    near = (near.astype(jnp.float32) + far.astype(jnp.float32)).astype(jnp.bfloat16)
    peer = lax.ppermute(near[members:], "dp", side)
    near = (near[:members].astype(jnp.float32) + peer.astype(jnp.float32)).astype(jnp.bfloat16)
    parts = [near[0]] + [
        lax.ppermute(near[i + 1], "expert", back[k]) for i, k in enumerate(shifts)
    ]
    return pl.pallas_call(
        final_kernel,
        out_shape=jax.ShapeDtypeStruct(residual.shape, jnp.bfloat16),
        in_specs=[VMEM] * (1 + members),
        out_specs=VMEM,
    )(mixed, *parts)


def solution(mesh):
    placed = (
        P(("replica", "expert", "dp"), None, None),
        P(("replica", "expert", "dp"), None, None),
        P(("replica", "expert", "dp"), None, None),
        P(("replica", "expert", "dp"), None, None),
        P(("replica", "expert", "dp"), None, None),
        P(("replica", "expert", "dp")),
        P(("replica", "expert", "dp"), None),
        P(("replica", "expert", "dp"), None, None),
        P(),
        P(("replica", "expert", "dp"), None, None),
        P(("replica", "expert", "dp"), None, None),
        P("expert", None, "dp"),
        P("expert", None, "dp"),
        P("expert", "dp", None),
    )
    near = mesh.shape["expert"] == 4 and mesh.shape["dp"] == 4
    return jax.shard_map(
        gathered if near else shards,
        mesh=mesh,
        in_specs=placed,
        out_specs=P(("replica", "expert", "dp"), None, None),
        check_vma=False,
    )
```

```python
import functools
import math

import jax
import jax.numpy as jnp
from jax import lax
from jax.experimental import pallas as pl
from jax.experimental.pallas import tpu as pltpu
from jax.sharding import PartitionSpec as P

HEAD_DIM = 128
TOP = 8
CAP = 2


THETA = 5000000.0
EPS = 1e-06
MASKED = -1e30


def rotate(vectors, where):
    half = vectors.shape[-1] // 2
    freq = THETA ** (-2.0 * jnp.arange(half, dtype=jnp.float32) / vectors.shape[-1])
    angle = where[..., None] * freq
    cosine = jnp.cos(angle)
    sine = jnp.sin(angle)
    first = vectors[..., :half]
    second = vectors[..., half:]
    return jnp.concatenate(
        [first * cosine - second * sine, second * cosine + first * sine], axis=-1
    )


def attend(queries, new_keys, new_values, cache_keys, cache_values, lengths, image_grid):
    count = queries.shape[0]
    steps = queries.shape[1]
    ctx = cache_keys.shape[1]
    kv_count = cache_keys.shape[2] // HEAD_DIM
    group = queries.shape[2] // HEAD_DIM // kv_count
    base = (
        lengths
        - image_grid[:, 0] * image_grid[:, 1]
        + jnp.maximum(image_grid[:, 0], image_grid[:, 1])
    )
    where = (base[:, None] + jnp.arange(steps, dtype=jnp.int32)[None, :]).astype(jnp.float32)
    query = rotate(
        queries.astype(jnp.float32).reshape(count, steps, kv_count, group, HEAD_DIM),
        where[:, :, None, None],
    )
    fresh = rotate(
        new_keys.astype(jnp.float32).reshape(count, steps, kv_count, HEAD_DIM), where[:, :, None]
    )
    cached = cache_keys.astype(jnp.float32).reshape(count, ctx, kv_count, HEAD_DIM)
    scale = 1.0 / math.sqrt(HEAD_DIM)
    old_scores = (
        jnp.einsum("rsgqd,rcgd->rsgqc", query, cached, precision=lax.Precision.HIGHEST) * scale
    )
    new_scores = (
        jnp.einsum("rsgqd,rtgd->rsgqt", query, fresh, precision=lax.Precision.HIGHEST) * scale
    )
    live = jnp.arange(ctx, dtype=jnp.int32)[None, :] < lengths[:, None]
    old_scores = jnp.where(live[:, None, None, None, :], old_scores, MASKED)
    causal = (
        jnp.arange(steps, dtype=jnp.int32)[None, :] <= jnp.arange(steps, dtype=jnp.int32)[:, None]
    )
    new_scores = jnp.where(causal[None, :, None, None, :], new_scores, MASKED)
    scores = jnp.concatenate([old_scores, new_scores], axis=-1)
    top = jnp.max(scores, axis=-1, keepdims=True)
    weights = jnp.exp(scores - top)
    probs = (weights / jnp.sum(weights, axis=-1, keepdims=True)).astype(jnp.bfloat16)
    values = jnp.concatenate(
        [
            cache_values.reshape(count, ctx, kv_count, HEAD_DIM),
            new_values.reshape(count, steps, kv_count, HEAD_DIM),
        ],
        axis=1,
    )
    out = jnp.einsum("rsgqc,rcgd->rsgqd", probs, values, preferred_element_type=jnp.float32)
    return out.astype(jnp.bfloat16).reshape(count, steps, -1)


def shards(
    queries,
    new_keys,
    new_values,
    cache_keys,
    cache_values,
    lengths,
    image_grid,
    residual,
    norm_gain,
    routes,
    route_gains,
    w_gate,
    w_up,
    w_down,
):
    rows, steps, width = residual.shape
    attended = attend(queries, new_keys, new_values, cache_keys, cache_values, lengths, image_grid)
    mixed = residual.astype(jnp.float32) + attended.astype(jnp.float32)
    normed = (
        mixed
        * lax.rsqrt(jnp.mean(mixed * mixed, axis=-1, keepdims=True) + EPS)
        * norm_gain.astype(jnp.float32)
    ).astype(jnp.bfloat16)
    shares = (route_gains / jnp.sum(route_gains, axis=-1, keepdims=True)).astype(jnp.bfloat16)
    members = lax.axis_size("expert")
    local = w_gate.shape[0]
    places = members * CAP * local
    picks = routes.reshape(-1)
    onehot = (picks[:, None] == jnp.arange(members * local, dtype=jnp.int32)[None, :]).astype(
        jnp.int32
    )
    earlier = jnp.sum((jnp.cumsum(onehot, axis=0) - onehot) * onehot, axis=1)
    target = picks // local * (CAP * local) + earlier * local + picks % local
    placed = (target[:, None] == jnp.arange(places, dtype=jnp.int32)[None, :]).reshape(
        rows * steps, TOP, places
    )
    chooser = jnp.sum(placed.astype(jnp.float32), axis=1).astype(jnp.bfloat16)
    weigher = jnp.sum(
        jnp.where(
            placed, shares.reshape(rows * steps, TOP, 1).astype(jnp.float32), jnp.float32(0.0)
        ),
        axis=1,
    ).astype(jnp.bfloat16)
    outgoing = jnp.einsum(
        "jp,jd->pd",
        chooser,
        normed.reshape(rows * steps, width),
        preferred_element_type=jnp.float32,
    )
    outgoing = outgoing.astype(jnp.bfloat16).reshape(members, CAP, local, width)
    incoming = lax.all_to_all(outgoing, "expert", split_axis=0, concat_axis=0, tiled=True)
    flat = incoming.reshape(-1, local, width)
    piece = lax.all_gather(flat, "dp", axis=0, tiled=True)
    gate = jnp.einsum("red,edh->reh", piece, w_gate, preferred_element_type=jnp.float32)
    upper = jnp.einsum("red,edh->reh", piece, w_up, preferred_element_type=jnp.float32)
    hidden = (jax.nn.silu(gate) * upper).astype(jnp.bfloat16)
    piece = hidden
    result = lax.psum_scatter(
        jnp.einsum("reh,ehd->red", piece, w_down, preferred_element_type=jnp.float32).astype(
            jnp.bfloat16
        ),
        "dp",
        scatter_dimension=0,
        tiled=True,
    )
    returned = lax.all_to_all(
        result.reshape(incoming.shape), "expert", split_axis=0, concat_axis=0, tiled=True
    )
    routed = jnp.dot(weigher, returned.reshape(places, width), preferred_element_type=jnp.float32)
    layer_out = mixed.reshape(rows * steps, width) + routed
    return layer_out.astype(jnp.bfloat16).reshape(rows, steps, width)


VMEM = pl.BlockSpec(memory_space=pltpu.VMEM)
SMEM = pl.BlockSpec(memory_space=pltpu.SMEM)
LANES = 128
VMEM_BYTES = 32 * 2**20
MAIN = 8


def stack(parts, axis=0):
    return jnp.concatenate(parts, axis=axis)


def front_kernel(
    q_ref, nk_ref, nv_ref, ck_ref, cv_ref, len_ref, grid_ref, res_ref, gain_ref, routes_ref,
    gains_ref, pay_ref, mixed_ref,
):
    rows, steps, width = q_ref.shape
    ctx = ck_ref.shape[1]
    kv_count = ck_ref.shape[2] // HEAD_DIM
    group = width // HEAD_DIM // kv_count
    half = HEAD_DIM // 2
    tall = group * steps
    fresh_pad = 8
    keys = ctx + fresh_pad
    lane = lax.broadcasted_iota(jnp.int32, (8, HEAD_DIM), 1)
    freq = jnp.exp((lane % half).astype(jnp.float32) * (-2.0 * math.log(THETA) / HEAD_DIM))
    sub = lax.broadcasted_iota(jnp.int32, (8, HEAD_DIM), 0)
    flip = jnp.where(lane < half, -1.0, 1.0)
    head_step = lax.broadcasted_iota(jnp.int32, (tall, keys), 0) % steps
    column = lax.broadcasted_iota(jnp.int32, (tall, keys), 1)
    fresh_live = (column >= ctx) & (column - ctx <= head_step)
    scale = 1.0 / math.sqrt(HEAD_DIM)

    def turn(vectors, cosine, sine):
        return vectors * cosine + pltpu.roll(vectors, half, 1) * sine

    gain = gain_ref[...].astype(jnp.float32).reshape(1, width)
    normed = []
    for r in range(rows):
        length = len_ref[r]
        high, wide = grid_ref[0, r], grid_ref[1, r]
        base = length - high * wide + jnp.maximum(high, wide)
        angle = (base + sub % steps).astype(jnp.float32) * freq
        cosine = jnp.cos(angle)
        sine = jnp.sin(angle) * flip
        cosines = stack([cosine] * (tall // 8))
        sines = stack([sine] * (tall // 8))
        live = (column < jnp.minimum(length, ctx)) | fresh_live
        q_r = q_ref[r].astype(jnp.float32)
        nk_r = nk_ref[r].astype(jnp.float32)
        nv_r = nv_ref[r].astype(jnp.float32)
        ck_r = ck_ref[r].astype(jnp.float32)
        cv_r = cv_ref[r].astype(jnp.float32)
        blank = jnp.zeros((fresh_pad - steps, HEAD_DIM), jnp.float32)
        pieces = []
        for g in range(kv_count):
            cols = slice(g * HEAD_DIM, (g + 1) * HEAD_DIM)
            first = g * group
            query = stack(
                [q_r[:, (first + h) * HEAD_DIM : (first + h + 1) * HEAD_DIM] for h in range(group)]
            )
            query = turn(query, cosines, sines)
            fresh = turn(stack([nk_r[:, cols], blank]), cosine, sine)
            key = stack([ck_r[:, cols], fresh])
            scores = (
                lax.dot_general(
                    query, key, (((1,), (1,)), ((), ())),
                    precision=lax.Precision.HIGHEST, preferred_element_type=jnp.float32,
                )
                * scale
            )
            scores = jnp.where(live, scores, MASKED)
            top = jnp.max(scores, axis=-1, keepdims=True)
            weights = jnp.exp(scores - top)
            probs = (weights / jnp.sum(weights, axis=-1, keepdims=True)).astype(jnp.bfloat16)
            value = stack([cv_r[:, cols], nv_r[:, cols], blank]).astype(jnp.bfloat16)
            out = jnp.dot(probs, value, preferred_element_type=jnp.float32)
            out = out.astype(jnp.bfloat16).astype(jnp.float32)
            pieces += [out[h * steps : (h + 1) * steps] for h in range(group)]
        mixed = res_ref[r].astype(jnp.float32) + stack(pieces, axis=1)
        mixed_ref[r] = mixed
        mean = jnp.mean(mixed * mixed, axis=-1, keepdims=True)
        normed.append(mixed * lax.rsqrt(mean + EPS) * gain)

    whole = MAIN // steps
    fold = width // 2
    pay_ref[:, :width] = stack(normed[:whole]).astype(pay_ref.dtype)
    late = normed[whole:]
    pay_ref[:, width : width + fold] = stack(
        [n[:, :fold] for n in late] + [n[:, fold:] for n in late]
    ).astype(pay_ref.dtype)

    place = lax.broadcasted_iota(jnp.int32, (steps, LANES), 1)
    spread = []
    for r in range(rows):
        gains = gains_ref[r]
        shares = gains / jnp.sum(gains, axis=-1, keepdims=True)
        picks = routes_ref[r] + (0 if r < whole else LANES // 2)
        dense = jnp.zeros((steps, LANES), jnp.float32)
        for k in range(TOP):
            dense = jnp.where(place == picks[:, k : k + 1], shares[:, k : k + 1], dense)
        spread.append(dense)
    early = stack(spread[:whole])
    late = stack(spread[whole:] + [jnp.zeros((MAIN - (rows - whole) * steps, LANES), jnp.float32)])
    pay_ref[:, width + fold :] = (early + late).astype(pay_ref.dtype)


def front(queries, new_keys, new_values, cache_keys, cache_values, lengths, image_grid, residual,
          norm_gain, routes, route_gains):
    rows, steps, width = queries.shape
    return pl.pallas_call(
        front_kernel,
        out_shape=(
            pltpu.VMEM((MAIN, width + width // 2 + LANES), jnp.bfloat16),
            pltpu.VMEM((rows, steps, width), jnp.float32),
        ),
        in_specs=[VMEM] * 5 + [SMEM] * 2 + [VMEM] * 4,
        out_specs=(VMEM, VMEM),
        cost_estimate=pl.CostEstimate(flops=10**7, bytes_accessed=10**6, transcendentals=10**4),
    )(queries, new_keys, new_values, cache_keys, cache_values, lengths, image_grid.T, residual,
      norm_gain, routes, route_gains)


SPLIT = 3584
GROUP = 4
CUT = 512


def fetch_kernel(parts, start, *refs):
    sources, (_, *outs, sem) = refs[:parts], refs[parts:]
    copies = [
        pltpu.make_async_copy(source.at[start + e], out.at[e], sem.at[p, e])
        for p, (source, out) in enumerate(zip(sources, outs))
        for e in range(out.shape[0])
    ]
    for copy in copies:
        copy.start()
    for copy in copies:
        copy.wait()


def fetch(weights, start, count, after):
    size = weights[0].size * 2 // weights[0].shape[0] * count * len(weights)
    place = pl.BlockSpec(memory_space=pl.ANY)
    shape = (count, *weights[0].shape[1:])
    return pl.pallas_call(
        functools.partial(fetch_kernel, len(weights), start),
        out_shape=[pltpu.VMEM(shape, jnp.bfloat16)] * len(weights),
        in_specs=[place] * (len(weights) + 1),
        out_specs=[VMEM] * len(weights),
        scratch_shapes=[pltpu.SemaphoreType.DMA((len(weights), count))],
        compiler_params=pltpu.CompilerParams(vmem_limit_bytes=2**20),
        cost_estimate=pl.CostEstimate(flops=0, bytes_accessed=size, transcendentals=0),
    )(*[pltpu.with_memory_space_constraint(w, pltpu.HBM) for w in weights], after)


def experts_kernel(blocks, axis, *refs):
    pays = refs[:blocks]
    (
        _, _, _, _, gate_hbm, up_hbm, down_hbm, near_ref, far_ref, gate_a, up_a, gate_b, up_b,
        held_ref, x_ref, share_ref, hidden_ref, held_sem, down_sem,
    ) = refs[blocks:]
    early = (gate_a, up_a, gate_b, up_b)
    local, quarter, width = gate_hbm.shape
    fold = width // 2
    rest = 4
    tokens = blocks * (MAIN + rest)
    tall = GROUP * quarter
    groups = local // GROUP
    ready = len(early) // 2

    def load(g):
        return [
            pltpu.make_async_copy(
                source.at[g * GROUP + k], held_ref.at[g - ready, p, k], held_sem.at[g - ready, p, k]
            )
            for p, source in enumerate((gate_hbm, up_hbm))
            for k in range(GROUP)
        ]

    cuts = fold // CUT

    def load_down(c):
        return [
            pltpu.make_async_copy(
                down_hbm.at[pl.ds(q * GROUP, GROUP), :, pl.ds(side * fold + c * CUT, CUT)],
                early[q].at[:, :, pl.ds(side * fold + c * CUT, CUT)],
                down_sem.at[c, q, side],
            )
            for q in range(groups)
            for side in range(2)
        ]

    for g in range(ready, groups):
        for copy in load(g):
            copy.start()

    spread = []
    for i in range(0, blocks, 2):
        pair = [pays[i + j][...].astype(jnp.float32) for j in range(2)]
        x_ref[i * MAIN : (i + 2) * MAIN] = stack([p[:, :width] for p in pair]).astype(x_ref.dtype)
        spread += [p[:, width + fold :] for p in pair]
    for i in range(0, blocks, 4):
        start = blocks * MAIN + i * rest
        four = [pays[i + j][...].astype(jnp.float32) for j in range(4)]
        left = stack([p[:rest, width : width + fold] for p in four])
        right = stack([p[rest:, width : width + fold] for p in four])
        x_ref[start : start + 4 * rest, :fold] = left.astype(x_ref.dtype)
        x_ref[start : start + 4 * rest, fold:] = right.astype(x_ref.dtype)
        spread += [p[:rest, width + fold :] for p in four]
    shares = stack(spread).T
    column = lax.broadcasted_iota(jnp.int32, (LANES // 2, tokens), 1)
    share_ref[...] = jnp.where(
        column < blocks * MAIN, shares[: LANES // 2], shares[LANES // 2 :]
    )
    first = lax.axis_index(axis) * local

    flat = (((1,), (1,)), ((), ()))

    def finish(g, gate, upper):
        hidden = jax.nn.silu(gate) * upper
        weight = stack(
            [
                jnp.broadcast_to(share_ref[pl.ds(first + g * GROUP + k, 1)], (quarter, tokens))
                for k in range(GROUP)
            ]
        )
        hidden_ref[:, g * tall : (g + 1) * tall] = (hidden * weight).T.astype(hidden_ref.dtype)

    made = None
    for g in range(groups):
        if g >= ready:
            for copy in load(g):
                copy.wait()
            few = -(-cuts // (groups - ready))
            for c in range((g - ready) * few, min((g - ready + 1) * few, cuts)):
                for copy in load_down(c):
                    copy.start()
        if g < ready:
            gate_at, up_at = early[2 * g], early[2 * g + 1]
        else:
            gate_at, up_at = held_ref.at[g - ready, 0], held_ref.at[g - ready, 1]
        gate, upper = [
            lax.dot_general(
                at[...].reshape(tall, width), x_ref[...], flat, preferred_element_type=jnp.float32
            )
            for at in (gate_at, up_at)
        ]
        if made is not None:
            finish(g - 1, *made)
        made = gate, upper
    for c in range(cuts):
        at = c * CUT
        for copy in load_down(c):
            copy.wait()
        if c == 0:
            finish(groups - 1, *made)
        low, high = [
            sum(
                jnp.dot(
                    hidden_ref[:, q * tall : (q + 1) * tall],
                    early[q][:, :, c : c + CUT].reshape(tall, CUT),
                    preferred_element_type=jnp.float32,
                )
                for q in range(groups)
            )
            for c in (at, fold + at)
        ]
        for b in range(blocks):
            out = near_ref if b < blocks // 2 else far_ref
            to = b % (blocks // 2)
            main = slice(b * MAIN, (b + 1) * MAIN)
            out[to, :, at : at + CUT] = low[main].astype(out.dtype)
            out[to, :, fold + at : fold + at + CUT] = high[main].astype(out.dtype)
            start = blocks * MAIN + b * rest
            late = stack([low[start : start + rest], high[start : start + rest]])
            out[to, :, width + at : width + at + CUT] = late.astype(out.dtype)


def experts(pays, early, w_gate, w_up, w_down, axis):
    blocks = len(pays)
    local, quarter, width = w_down.shape
    tokens = blocks * 12
    packed = width + width // 2
    half = pltpu.VMEM((blocks // 2, MAIN, packed), jnp.bfloat16)
    place = pl.BlockSpec(memory_space=pl.ANY)
    held = [pltpu.with_memory_space_constraint(a, pltpu.VMEM) for a in (*pays, *early)]
    return pl.pallas_call(
        functools.partial(experts_kernel, blocks, axis),
        out_shape=[half, half] + [pltpu.VMEM(a.shape, a.dtype) for a in early],
        in_specs=[VMEM] * len(held) + [place] * 3,
        out_specs=[VMEM] * (2 + len(early)),
        input_output_aliases={blocks + i: 2 + i for i in range(len(early))},
        scratch_shapes=[
            pltpu.VMEM((local // GROUP - 2, 2, GROUP, quarter, width), jnp.bfloat16),
            pltpu.VMEM((tokens, width), jnp.bfloat16),
            pltpu.VMEM((LANES // 2, tokens), jnp.float32),
            pltpu.VMEM((tokens, local * quarter), jnp.bfloat16),
            pltpu.SemaphoreType.DMA((local // GROUP - 2, 2, GROUP)),
            pltpu.SemaphoreType.DMA((width // 2 // CUT, local // GROUP, 2)),
        ],
        compiler_params=pltpu.CompilerParams(vmem_limit_bytes=VMEM_BYTES),
        cost_estimate=pl.CostEstimate(
            flops=6 * tokens * local * quarter * width,
            bytes_accessed=4 * local * quarter * width,
            transcendentals=tokens * local * quarter,
        ),
    )(*held, *[pltpu.with_memory_space_constraint(w, pltpu.HBM) for w in (w_gate, w_up, w_down)])[:2]


def final_kernel(mixed_ref, *refs):
    parts, out_ref = refs[:-1], refs[-1]
    rows, steps, width = mixed_ref.shape
    fold = width // 2
    total = parts[0][...].astype(jnp.float32)
    for part in parts[1:]:
        total = total + part[...].astype(jnp.float32)
    for r in range(rows):
        at = r * steps
        if at < MAIN:
            routed = total[at : at + steps, :width]
        else:
            at -= MAIN
            low = total[at : at + steps, width:]
            at += MAIN // 2
            routed = stack([low, total[at : at + steps, width:]], axis=1)
        out_ref[r] = (mixed_ref[r] + routed).astype(out_ref.dtype)


def gathered(
    queries, new_keys, new_values, cache_keys, cache_values, lengths, image_grid, residual,
    norm_gain, routes, route_gains, w_gate, w_up, w_down,
):
    members = lax.axis_size("expert")
    pay, mixed = front(
        queries, new_keys, new_values, cache_keys, cache_values, lengths, image_grid, residual,
        norm_gain, routes, route_gains,
    )
    twin = [(0, 1), (1, 0), (2, 3), (3, 2)]
    side = [(0, 2), (2, 0), (1, 3), (3, 1)]
    shifts = (2, 1, 3)
    ahead = {k: [(i, (i + k) % members) for i in range(members)] for k in shifts}
    back = {k: [(i, (i - k) % members) for i in range(members)] for k in shifts}
    line = [pay] + [lax.ppermute(pay, "expert", ahead[k]) for k in shifts]
    gate, up = jnp.swapaxes(w_gate, 1, 2), jnp.swapaxes(w_up, 1, 2)
    pair = fetch((gate, up), 0, GROUP, pay)
    line[1], *pair = lax.optimization_barrier((line[1], *pair))
    pays = line + [lax.ppermute(p, "dp", side) for p in line]
    second = fetch((gate, up), GROUP, GROUP, line[-1])
    *x_side, first_two, next_two = lax.optimization_barrier((*pays[members:], *second))
    second = [first_two, next_two]
    pays = pays[:members] + x_side
    pays = pays + [lax.ppermute(p, "dp", twin) for p in pays]
    near, far = experts(pays, (*pair, *second), gate, up, w_down, "expert")
    far = lax.ppermute(far, "dp", twin)
    near = (near.astype(jnp.float32) + far.astype(jnp.float32)).astype(jnp.bfloat16)
    own, other = near[:members], near[members:]
    peer = lax.ppermute(other[1:, :, :SPLIT], "dp", side)
    lines = [
        lax.ppermute(other[i + 1, :, SPLIT:], "expert", back[k]) for i, k in enumerate(shifts)
    ]
    first = own[1:, :, :SPLIT].astype(jnp.float32) + peer.astype(jnp.float32)
    own_line = stack([first.astype(jnp.bfloat16), own[1:, :, SPLIT:]], axis=2)
    parts = [own[0]] + [
        lax.ppermute(own_line[i], "expert", back[k]) for i, k in enumerate(shifts)
    ]
    last = other[0, :, SPLIT:].astype(jnp.float32) + sum(p.astype(jnp.float32) for p in lines)
    crossed = stack([other[0, :, :SPLIT], last.astype(jnp.bfloat16)], axis=1)
    parts.append(lax.ppermute(crossed, "dp", side))
    return pl.pallas_call(
        final_kernel,
        out_shape=jax.ShapeDtypeStruct(residual.shape, jnp.bfloat16),
        in_specs=[VMEM] * (1 + len(parts)),
        out_specs=VMEM,
    )(*[pltpu.with_memory_space_constraint(a, pltpu.VMEM) for a in (mixed, *parts)])


def solution(mesh):
    placed = (
        P(("replica", "expert", "dp"), None, None),
        P(("replica", "expert", "dp"), None, None),
        P(("replica", "expert", "dp"), None, None),
        P(("replica", "expert", "dp"), None, None),
        P(("replica", "expert", "dp"), None, None),
        P(("replica", "expert", "dp")),
        P(("replica", "expert", "dp"), None),
        P(("replica", "expert", "dp"), None, None),
        P(),
        P(("replica", "expert", "dp"), None, None),
        P(("replica", "expert", "dp"), None, None),
        P("expert", None, "dp"),
        P("expert", None, "dp"),
        P("expert", "dp", None),
    )
    near = mesh.shape["expert"] == 4 and mesh.shape["dp"] == 4
    return jax.shard_map(
        gathered if near else shards,
        mesh=mesh,
        in_specs=placed,
        out_specs=P(("replica", "expert", "dp"), None, None),
        check_vma=False,
    )
```

```python
import functools
import math

import jax
import jax.numpy as jnp
from jax import lax
from jax.experimental import pallas as pl
from jax.experimental.pallas import tpu as pltpu
from jax.sharding import PartitionSpec as P

HEAD_DIM = 128
TOP = 8
CAP = 2


THETA = 5000000.0
EPS = 1e-06
MASKED = -1e30


def rotate(vectors, where):
    half = vectors.shape[-1] // 2
    freq = THETA ** (-2.0 * jnp.arange(half, dtype=jnp.float32) / vectors.shape[-1])
    angle = where[..., None] * freq
    cosine = jnp.cos(angle)
    sine = jnp.sin(angle)
    first = vectors[..., :half]
    second = vectors[..., half:]
    return jnp.concatenate(
        [first * cosine - second * sine, second * cosine + first * sine], axis=-1
    )


def attend(queries, new_keys, new_values, cache_keys, cache_values, lengths, image_grid):
    count = queries.shape[0]
    steps = queries.shape[1]
    ctx = cache_keys.shape[1]
    kv_count = cache_keys.shape[2] // HEAD_DIM
    group = queries.shape[2] // HEAD_DIM // kv_count
    base = (
        lengths
        - image_grid[:, 0] * image_grid[:, 1]
        + jnp.maximum(image_grid[:, 0], image_grid[:, 1])
    )
    where = (base[:, None] + jnp.arange(steps, dtype=jnp.int32)[None, :]).astype(jnp.float32)
    query = rotate(
        queries.astype(jnp.float32).reshape(count, steps, kv_count, group, HEAD_DIM),
        where[:, :, None, None],
    )
    fresh = rotate(
        new_keys.astype(jnp.float32).reshape(count, steps, kv_count, HEAD_DIM), where[:, :, None]
    )
    cached = cache_keys.astype(jnp.float32).reshape(count, ctx, kv_count, HEAD_DIM)
    scale = 1.0 / math.sqrt(HEAD_DIM)
    old_scores = (
        jnp.einsum("rsgqd,rcgd->rsgqc", query, cached, precision=lax.Precision.HIGHEST) * scale
    )
    new_scores = (
        jnp.einsum("rsgqd,rtgd->rsgqt", query, fresh, precision=lax.Precision.HIGHEST) * scale
    )
    live = jnp.arange(ctx, dtype=jnp.int32)[None, :] < lengths[:, None]
    old_scores = jnp.where(live[:, None, None, None, :], old_scores, MASKED)
    causal = (
        jnp.arange(steps, dtype=jnp.int32)[None, :] <= jnp.arange(steps, dtype=jnp.int32)[:, None]
    )
    new_scores = jnp.where(causal[None, :, None, None, :], new_scores, MASKED)
    scores = jnp.concatenate([old_scores, new_scores], axis=-1)
    top = jnp.max(scores, axis=-1, keepdims=True)
    weights = jnp.exp(scores - top)
    probs = (weights / jnp.sum(weights, axis=-1, keepdims=True)).astype(jnp.bfloat16)
    values = jnp.concatenate(
        [
            cache_values.reshape(count, ctx, kv_count, HEAD_DIM),
            new_values.reshape(count, steps, kv_count, HEAD_DIM),
        ],
        axis=1,
    )
    out = jnp.einsum("rsgqc,rcgd->rsgqd", probs, values, preferred_element_type=jnp.float32)
    return out.astype(jnp.bfloat16).reshape(count, steps, -1)


def shards(
    queries,
    new_keys,
    new_values,
    cache_keys,
    cache_values,
    lengths,
    image_grid,
    residual,
    norm_gain,
    routes,
    route_gains,
    w_gate,
    w_up,
    w_down,
):
    rows, steps, width = residual.shape
    attended = attend(queries, new_keys, new_values, cache_keys, cache_values, lengths, image_grid)
    mixed = residual.astype(jnp.float32) + attended.astype(jnp.float32)
    normed = (
        mixed
        * lax.rsqrt(jnp.mean(mixed * mixed, axis=-1, keepdims=True) + EPS)
        * norm_gain.astype(jnp.float32)
    ).astype(jnp.bfloat16)
    shares = (route_gains / jnp.sum(route_gains, axis=-1, keepdims=True)).astype(jnp.bfloat16)
    members = lax.axis_size("expert")
    local = w_gate.shape[0]
    places = members * CAP * local
    picks = routes.reshape(-1)
    onehot = (picks[:, None] == jnp.arange(members * local, dtype=jnp.int32)[None, :]).astype(
        jnp.int32
    )
    earlier = jnp.sum((jnp.cumsum(onehot, axis=0) - onehot) * onehot, axis=1)
    target = picks // local * (CAP * local) + earlier * local + picks % local
    placed = (target[:, None] == jnp.arange(places, dtype=jnp.int32)[None, :]).reshape(
        rows * steps, TOP, places
    )
    chooser = jnp.sum(placed.astype(jnp.float32), axis=1).astype(jnp.bfloat16)
    weigher = jnp.sum(
        jnp.where(
            placed, shares.reshape(rows * steps, TOP, 1).astype(jnp.float32), jnp.float32(0.0)
        ),
        axis=1,
    ).astype(jnp.bfloat16)
    outgoing = jnp.einsum(
        "jp,jd->pd",
        chooser,
        normed.reshape(rows * steps, width),
        preferred_element_type=jnp.float32,
    )
    outgoing = outgoing.astype(jnp.bfloat16).reshape(members, CAP, local, width)
    incoming = lax.all_to_all(outgoing, "expert", split_axis=0, concat_axis=0, tiled=True)
    flat = incoming.reshape(-1, local, width)
    piece = lax.all_gather(flat, "dp", axis=0, tiled=True)
    gate = jnp.einsum("red,edh->reh", piece, w_gate, preferred_element_type=jnp.float32)
    upper = jnp.einsum("red,edh->reh", piece, w_up, preferred_element_type=jnp.float32)
    hidden = (jax.nn.silu(gate) * upper).astype(jnp.bfloat16)
    piece = hidden
    result = lax.psum_scatter(
        jnp.einsum("reh,ehd->red", piece, w_down, preferred_element_type=jnp.float32).astype(
            jnp.bfloat16
        ),
        "dp",
        scatter_dimension=0,
        tiled=True,
    )
    returned = lax.all_to_all(
        result.reshape(incoming.shape), "expert", split_axis=0, concat_axis=0, tiled=True
    )
    routed = jnp.dot(weigher, returned.reshape(places, width), preferred_element_type=jnp.float32)
    layer_out = mixed.reshape(rows * steps, width) + routed
    return layer_out.astype(jnp.bfloat16).reshape(rows, steps, width)


VMEM = pl.BlockSpec(memory_space=pltpu.VMEM)
SMEM = pl.BlockSpec(memory_space=pltpu.SMEM)
LANES = 128
VMEM_BYTES = 32 * 2**20
MAIN = 8


def stack(parts, axis=0):
    return jnp.concatenate(parts, axis=axis)


def front_kernel(
    q_ref, nk_ref, nv_ref, ck_ref, cv_ref, len_ref, grid_ref, res_ref, gain_ref, routes_ref,
    gains_ref, pay_ref, mixed_ref,
):
    rows, steps, width = q_ref.shape
    ctx = ck_ref.shape[1]
    kv_count = ck_ref.shape[2] // HEAD_DIM
    group = width // HEAD_DIM // kv_count
    half = HEAD_DIM // 2
    tall = group * steps
    fresh_pad = 8
    keys = ctx + fresh_pad
    lane = lax.broadcasted_iota(jnp.int32, (8, HEAD_DIM), 1)
    freq = jnp.exp((lane % half).astype(jnp.float32) * (-2.0 * math.log(THETA) / HEAD_DIM))
    sub = lax.broadcasted_iota(jnp.int32, (8, HEAD_DIM), 0)
    flip = jnp.where(lane < half, -1.0, 1.0)
    head_step = lax.broadcasted_iota(jnp.int32, (tall, keys), 0) % steps
    column = lax.broadcasted_iota(jnp.int32, (tall, keys), 1)
    fresh_live = (column >= ctx) & (column - ctx <= head_step)
    scale = 1.0 / math.sqrt(HEAD_DIM)

    def turn(vectors, cosine, sine):
        return vectors * cosine + pltpu.roll(vectors, half, 1) * sine

    gain = gain_ref[...].astype(jnp.float32).reshape(1, width)
    normed = []
    for r in range(rows):
        length = len_ref[r]
        high, wide = grid_ref[0, r], grid_ref[1, r]
        base = length - high * wide + jnp.maximum(high, wide)
        angle = (base + sub % steps).astype(jnp.float32) * freq
        cosine = jnp.cos(angle)
        sine = jnp.sin(angle) * flip
        cosines = stack([cosine] * (tall // 8))
        sines = stack([sine] * (tall // 8))
        live = (column < jnp.minimum(length, ctx)) | fresh_live
        q_r = q_ref[r].astype(jnp.float32)
        nk_r = nk_ref[r].astype(jnp.float32)
        nv_r = nv_ref[r].astype(jnp.float32)
        ck_r = ck_ref[r].astype(jnp.float32)
        cv_r = cv_ref[r].astype(jnp.float32)
        blank = jnp.zeros((fresh_pad - steps, HEAD_DIM), jnp.float32)
        pieces = []
        for g in range(kv_count):
            cols = slice(g * HEAD_DIM, (g + 1) * HEAD_DIM)
            first = g * group
            query = stack(
                [q_r[:, (first + h) * HEAD_DIM : (first + h + 1) * HEAD_DIM] for h in range(group)]
            )
            query = turn(query, cosines, sines)
            fresh = turn(stack([nk_r[:, cols], blank]), cosine, sine)
            key = stack([ck_r[:, cols], fresh])
            scores = (
                lax.dot_general(
                    query, key, (((1,), (1,)), ((), ())),
                    precision=lax.Precision.HIGHEST, preferred_element_type=jnp.float32,
                )
                * scale
            )
            scores = jnp.where(live, scores, MASKED)
            top = jnp.max(scores, axis=-1, keepdims=True)
            weights = jnp.exp(scores - top)
            probs = (weights / jnp.sum(weights, axis=-1, keepdims=True)).astype(jnp.bfloat16)
            value = stack([cv_r[:, cols], nv_r[:, cols], blank]).astype(jnp.bfloat16)
            out = jnp.dot(probs, value, preferred_element_type=jnp.float32)
            out = out.astype(jnp.bfloat16).astype(jnp.float32)
            pieces += [out[h * steps : (h + 1) * steps] for h in range(group)]
        mixed = res_ref[r].astype(jnp.float32) + stack(pieces, axis=1)
        mixed_ref[r] = mixed
        mean = jnp.mean(mixed * mixed, axis=-1, keepdims=True)
        normed.append(mixed * lax.rsqrt(mean + EPS) * gain)

    whole = MAIN // steps
    fold = width // 2
    pay_ref[:, :width] = stack(normed[:whole]).astype(pay_ref.dtype)
    late = normed[whole:]
    pay_ref[:, width : width + fold] = stack(
        [n[:, :fold] for n in late] + [n[:, fold:] for n in late]
    ).astype(pay_ref.dtype)

    place = lax.broadcasted_iota(jnp.int32, (steps, LANES), 1)
    spread = []
    for r in range(rows):
        gains = gains_ref[r]
        shares = gains / jnp.sum(gains, axis=-1, keepdims=True)
        picks = routes_ref[r] + (0 if r < whole else LANES // 2)
        dense = jnp.zeros((steps, LANES), jnp.float32)
        for k in range(TOP):
            dense = jnp.where(place == picks[:, k : k + 1], shares[:, k : k + 1], dense)
        spread.append(dense)
    early = stack(spread[:whole])
    late = stack(spread[whole:] + [jnp.zeros((MAIN - (rows - whole) * steps, LANES), jnp.float32)])
    pay_ref[:, width + fold :] = (early + late).astype(pay_ref.dtype)


def front(queries, new_keys, new_values, cache_keys, cache_values, lengths, image_grid, residual,
          norm_gain, routes, route_gains):
    rows, steps, width = queries.shape
    return pl.pallas_call(
        front_kernel,
        out_shape=(
            pltpu.VMEM((MAIN, width + width // 2 + LANES), jnp.bfloat16),
            pltpu.VMEM((rows, steps, width), jnp.float32),
        ),
        in_specs=[VMEM] * 5 + [SMEM] * 2 + [VMEM] * 4,
        out_specs=(VMEM, VMEM),
        cost_estimate=pl.CostEstimate(flops=10**7, bytes_accessed=10**6, transcendentals=10**4),
    )(queries, new_keys, new_values, cache_keys, cache_values, lengths, image_grid.T, residual,
      norm_gain, routes, route_gains)


SPLIT = 3072
GROUP = 4
CUT = 512


def fetch_kernel(parts, start, *refs):
    sources, (_, *outs, sem) = refs[:parts], refs[parts:]
    copies = [
        pltpu.make_async_copy(source.at[start + e], out.at[e], sem.at[p, e])
        for p, (source, out) in enumerate(zip(sources, outs))
        for e in range(out.shape[0])
    ]
    for copy in copies:
        copy.start()
    for copy in copies:
        copy.wait()


def fetch(weights, start, count, after):
    size = weights[0].size * 2 // weights[0].shape[0] * count * len(weights)
    place = pl.BlockSpec(memory_space=pl.ANY)
    shape = (count, *weights[0].shape[1:])
    return pl.pallas_call(
        functools.partial(fetch_kernel, len(weights), start),
        out_shape=[pltpu.VMEM(shape, jnp.bfloat16)] * len(weights),
        in_specs=[place] * (len(weights) + 1),
        out_specs=[VMEM] * len(weights),
        scratch_shapes=[pltpu.SemaphoreType.DMA((len(weights), count))],
        compiler_params=pltpu.CompilerParams(vmem_limit_bytes=2**20),
        cost_estimate=pl.CostEstimate(flops=0, bytes_accessed=size, transcendentals=0),
    )(*[pltpu.with_memory_space_constraint(w, pltpu.HBM) for w in weights], after)


def experts_kernel(blocks, axis, *refs):
    pays = refs[:blocks]
    (
        _, _, _, _, gate_hbm, up_hbm, down_hbm, near_ref, far_ref, gate_a, up_a, gate_b, up_b,
        held_ref, x_ref, share_ref, hidden_ref, held_sem, down_sem,
    ) = refs[blocks:]
    early = (gate_a, up_a, gate_b, up_b)
    local, quarter, width = gate_hbm.shape
    fold = width // 2
    rest = 4
    tokens = blocks * (MAIN + rest)
    tall = GROUP * quarter
    groups = local // GROUP
    ready = len(early) // 2

    def load(g):
        return [
            pltpu.make_async_copy(
                source.at[g * GROUP + k], held_ref.at[g - ready, p, k], held_sem.at[g - ready, p, k]
            )
            for p, source in enumerate((gate_hbm, up_hbm))
            for k in range(GROUP)
        ]

    cuts = fold // CUT

    def load_down(c):
        return [
            pltpu.make_async_copy(
                down_hbm.at[pl.ds(q * GROUP, GROUP), :, pl.ds(side * fold + c * CUT, CUT)],
                early[q].at[:, :, pl.ds(side * fold + c * CUT, CUT)],
                down_sem.at[c, q, side],
            )
            for q in range(groups)
            for side in range(2)
        ]

    for g in range(ready, groups):
        for copy in load(g):
            copy.start()

    spread = []
    for i in range(0, blocks, 2):
        pair = [pays[i + j][...].astype(jnp.float32) for j in range(2)]
        x_ref[i * MAIN : (i + 2) * MAIN] = stack([p[:, :width] for p in pair]).astype(x_ref.dtype)
        spread += [p[:, width + fold :] for p in pair]
    for i in range(0, blocks, 4):
        start = blocks * MAIN + i * rest
        four = [pays[i + j][...].astype(jnp.float32) for j in range(4)]
        left = stack([p[:rest, width : width + fold] for p in four])
        right = stack([p[rest:, width : width + fold] for p in four])
        x_ref[start : start + 4 * rest, :fold] = left.astype(x_ref.dtype)
        x_ref[start : start + 4 * rest, fold:] = right.astype(x_ref.dtype)
        spread += [p[:rest, width + fold :] for p in four]
    shares = stack(spread).T
    column = lax.broadcasted_iota(jnp.int32, (LANES // 2, tokens), 1)
    share_ref[...] = jnp.where(
        column < blocks * MAIN, shares[: LANES // 2], shares[LANES // 2 :]
    )
    first = lax.axis_index(axis) * local

    flat = (((1,), (1,)), ((), ()))

    def finish(g, gate, upper):
        hidden = jax.nn.silu(gate) * upper
        weight = stack(
            [
                jnp.broadcast_to(share_ref[pl.ds(first + g * GROUP + k, 1)], (quarter, tokens))
                for k in range(GROUP)
            ]
        )
        hidden_ref[:, g * tall : (g + 1) * tall] = (hidden * weight).T.astype(hidden_ref.dtype)

    made = None
    for g in range(groups):
        if g >= ready:
            for copy in load(g):
                copy.wait()
            few = -(-cuts // (groups - ready))
            for c in range((g - ready) * few, min((g - ready + 1) * few, cuts)):
                for copy in load_down(c):
                    copy.start()
        if g < ready:
            gate_at, up_at = early[2 * g], early[2 * g + 1]
        else:
            gate_at, up_at = held_ref.at[g - ready, 0], held_ref.at[g - ready, 1]
        gate, upper = [
            lax.dot_general(
                at[...].reshape(tall, width), x_ref[...], flat, preferred_element_type=jnp.float32
            )
            for at in (gate_at, up_at)
        ]
        if made is not None:
            finish(g - 1, *made)
        made = gate, upper
    for c in range(cuts):
        at = c * CUT
        for copy in load_down(c):
            copy.wait()
        if c == 0:
            finish(groups - 1, *made)
        low, high = [
            sum(
                jnp.dot(
                    hidden_ref[:, q * tall : (q + 1) * tall],
                    early[q][:, :, c : c + CUT].reshape(tall, CUT),
                    preferred_element_type=jnp.float32,
                )
                for q in range(groups)
            )
            for c in (at, fold + at)
        ]
        for b in range(blocks):
            out = near_ref if b < blocks // 2 else far_ref
            to = b % (blocks // 2)
            main = slice(b * MAIN, (b + 1) * MAIN)
            out[to, :, at : at + CUT] = low[main].astype(out.dtype)
            out[to, :, fold + at : fold + at + CUT] = high[main].astype(out.dtype)
            start = blocks * MAIN + b * rest
            late = stack([low[start : start + rest], high[start : start + rest]])
            out[to, :, width + at : width + at + CUT] = late.astype(out.dtype)


def experts(pays, early, w_gate, w_up, w_down, axis):
    blocks = len(pays)
    local, quarter, width = w_down.shape
    tokens = blocks * 12
    packed = width + width // 2
    half = pltpu.VMEM((blocks // 2, MAIN, packed), jnp.bfloat16)
    place = pl.BlockSpec(memory_space=pl.ANY)
    held = [pltpu.with_memory_space_constraint(a, pltpu.VMEM) for a in (*pays, *early)]
    return pl.pallas_call(
        functools.partial(experts_kernel, blocks, axis),
        out_shape=[half, half] + [pltpu.VMEM(a.shape, a.dtype) for a in early],
        in_specs=[VMEM] * len(held) + [place] * 3,
        out_specs=[VMEM] * (2 + len(early)),
        input_output_aliases={blocks + i: 2 + i for i in range(len(early))},
        scratch_shapes=[
            pltpu.VMEM((local // GROUP - 2, 2, GROUP, quarter, width), jnp.bfloat16),
            pltpu.VMEM((tokens, width), jnp.bfloat16),
            pltpu.VMEM((LANES // 2, tokens), jnp.float32),
            pltpu.VMEM((tokens, local * quarter), jnp.bfloat16),
            pltpu.SemaphoreType.DMA((local // GROUP - 2, 2, GROUP)),
            pltpu.SemaphoreType.DMA((width // 2 // CUT, local // GROUP, 2)),
        ],
        compiler_params=pltpu.CompilerParams(vmem_limit_bytes=VMEM_BYTES),
        cost_estimate=pl.CostEstimate(
            flops=6 * tokens * local * quarter * width,
            bytes_accessed=4 * local * quarter * width,
            transcendentals=tokens * local * quarter,
        ),
    )(*held, *[pltpu.with_memory_space_constraint(w, pltpu.HBM) for w in (w_gate, w_up, w_down)])[:2]


def final_kernel(mixed_ref, *refs):
    parts, out_ref = refs[:-1], refs[-1]
    rows, steps, width = mixed_ref.shape
    fold = width // 2
    total = parts[0][...].astype(jnp.float32)
    for part in parts[1:]:
        total = total + part[...].astype(jnp.float32)
    for r in range(rows):
        at = r * steps
        if at < MAIN:
            routed = total[at : at + steps, :width]
        else:
            at -= MAIN
            low = total[at : at + steps, width:]
            at += MAIN // 2
            routed = stack([low, total[at : at + steps, width:]], axis=1)
        out_ref[r] = (mixed_ref[r] + routed).astype(out_ref.dtype)


def gathered(
    queries, new_keys, new_values, cache_keys, cache_values, lengths, image_grid, residual,
    norm_gain, routes, route_gains, w_gate, w_up, w_down,
):
    members = lax.axis_size("expert")
    pay, mixed = front(
        queries, new_keys, new_values, cache_keys, cache_values, lengths, image_grid, residual,
        norm_gain, routes, route_gains,
    )
    twin = [(0, 1), (1, 0), (2, 3), (3, 2)]
    side = [(0, 2), (2, 0), (1, 3), (3, 1)]
    shifts = (2, 1, 3)
    ahead = {k: [(i, (i + k) % members) for i in range(members)] for k in shifts}
    back = {k: [(i, (i - k) % members) for i in range(members)] for k in shifts}
    line = [pay] + [lax.ppermute(pay, "expert", ahead[k]) for k in shifts]
    gate, up = jnp.swapaxes(w_gate, 1, 2), jnp.swapaxes(w_up, 1, 2)
    pair = fetch((gate, up), 0, GROUP, pay)
    line[1], *pair = lax.optimization_barrier((line[1], *pair))
    pays = line + [lax.ppermute(p, "dp", side) for p in line]
    second = fetch((gate, up), GROUP, GROUP, line[-1])
    *x_side, first_two, next_two = lax.optimization_barrier((*pays[members:], *second))
    second = [first_two, next_two]
    pays = pays[:members] + x_side
    pays = pays + [lax.ppermute(p, "dp", twin) for p in pays]
    near, far = experts(pays, (*pair, *second), gate, up, w_down, "expert")
    far = lax.ppermute(far, "dp", twin)
    near = (near.astype(jnp.float32) + far.astype(jnp.float32)).astype(jnp.bfloat16)
    own, other = near[:members], near[members:]
    peer = lax.ppermute(other[1:, :, :SPLIT], "dp", side)
    lines = [
        lax.ppermute(other[i + 1, :, SPLIT:], "expert", back[k]) for i, k in enumerate(shifts)
    ]
    first = own[1:, :, :SPLIT].astype(jnp.float32) + peer.astype(jnp.float32)
    own_line = stack([first.astype(jnp.bfloat16), own[1:, :, SPLIT:]], axis=2)
    parts = [own[0]] + [
        lax.ppermute(own_line[i], "expert", back[k]) for i, k in enumerate(shifts)
    ]
    last = other[0, :, SPLIT:].astype(jnp.float32) + sum(p.astype(jnp.float32) for p in lines)
    crossed = stack([other[0, :, :SPLIT], last.astype(jnp.bfloat16)], axis=1)
    parts.append(lax.ppermute(crossed, "dp", side))
    return pl.pallas_call(
        final_kernel,
        out_shape=jax.ShapeDtypeStruct(residual.shape, jnp.bfloat16),
        in_specs=[VMEM] * (1 + len(parts)),
        out_specs=VMEM,
    )(*[pltpu.with_memory_space_constraint(a, pltpu.VMEM) for a in (mixed, *parts)])


def solution(mesh):
    placed = (
        P(("replica", "expert", "dp"), None, None),
        P(("replica", "expert", "dp"), None, None),
        P(("replica", "expert", "dp"), None, None),
        P(("replica", "expert", "dp"), None, None),
        P(("replica", "expert", "dp"), None, None),
        P(("replica", "expert", "dp")),
        P(("replica", "expert", "dp"), None),
        P(("replica", "expert", "dp"), None, None),
        P(),
        P(("replica", "expert", "dp"), None, None),
        P(("replica", "expert", "dp"), None, None),
        P("expert", None, "dp"),
        P("expert", None, "dp"),
        P("expert", "dp", None),
    )
    near = mesh.shape["expert"] == 4 and mesh.shape["dp"] == 4
    return jax.shard_map(
        gathered if near else shards,
        mesh=mesh,
        in_specs=placed,
        out_specs=P(("replica", "expert", "dp"), None, None),
        check_vma=False,
    )
```
